128 devices in a mesh: section: 8 (over y_lo, z), dp: 16 (over y_hi, x, core).
Axes of the slice: x: 4, y: 4 (y_hi: 2, y_lo: 2; y = y_hi * 2 + y_lo), z: 4, core: 2. Of those that a mesh axis runs over, the one named last changes fastest.
Arguments:
- activations: bfloat16 [8, 2, 1536, 5120], P('section', None, 'dp'), may hold values from -1 to 1
- norm_gain: float32 [8, 5120], P('section'), may hold values from 0.1 to 1.9
- key_weight: bfloat16 [8, 5120, 512], P('section'), may hold values from -0.59765625 to 0.59765625
- key_gain: float32 [8, 128], P('section'), may hold values from 0.1 to 1.9
- key_cotangent: bfloat16 [8, 2, 1536, 512], P('section', None, 'dp'), may hold values from -2 to 2
- upstream: bfloat16 [2, 1536, 5120], P(None, 'dp'), may hold values from -3 to 3
- master: float32 [8, 5120, 512], P('section', 'dp'), may hold values from -0.6 to 0.6
- first_moment: float32 [8, 5120, 512], P('section', 'dp'), may hold values from -6 to 6
- second_moment: float32 [8, 5120, 512], P('section', 'dp'), may hold values from 1 to 30
Outputs:
- input_grad: bfloat16 [8, 2, 1536, 5120], P('section', None, 'dp')
- new_weight: bfloat16 [8, 5120, 512], P('section')
- new_master: float32 [8, 5120, 512], P('section', 'dp')
- new_first: float32 [8, 5120, 512], P('section', 'dp')
- new_second: float32 [8, 5120, 512], P('section', 'dp')
The draws below stay inside these ranges and needn't reach their ends.
All inputs are finite; a program needn't handle non-finite values.
Results may differ from the reference program's by a relative error of at most 0.0048.
Values may be sent and summed in bfloat16 or wider, within the bound.
No kernel may reach another device: no remote copies, remote signals or barrier semaphores. Data moves between devices by JAX's collectives and lax.ppermute only.
A program may use at most 128 MiB of HBM per device.

```python
import math
import jax
import jax.numpy as jnp
from jax import lax

D = 5120
HEAD = 128
HEADS_KV = 4
MB = 2
KV = 512
TOKENS = 1536
SECTIONS = 8


def block_levels(stream_key, extent, shards, smallest, largest):
    def one(axis_at, shards_of):
        steps = jax.random.uniform(jax.random.fold_in(jax.random.fold_in(stream_key, 6), axis_at), (shards_of,), jnp.float32, smallest / len(shards), largest / len(shards))
        return jnp.repeat(jnp.exp(steps), extent[axis_at] // shards_of).reshape((-1,) + (1,) * (len(extent) - axis_at - 1))

    loudness = one(*shards[0])
    for cut in shards[1:]:
        loudness = loudness * one(*cut)
    return loudness


def noise(own_key, extent, width, limit, cuts=(), dtype=jnp.bfloat16):
    level = block_levels(own_key, extent, cuts, -0.22, 0.18) if cuts else 1.0
    drawn = jax.random.normal(own_key, extent, jnp.float32) * width * level
    return jnp.minimum(jnp.maximum(drawn, -limit), limit).astype(dtype)


def setup_inputs(seed: int = 0) -> dict:
    key_of = jax.random.split(jax.random.key(seed), 10)
    return {
        "activations": noise(key_of[0], (SECTIONS, MB, TOKENS, D), 0.15, 1.0, ((0, 8), (2, 16))),
        "norm_gain": jnp.clip(1.0 + 0.18 * jax.random.normal(key_of[1], (SECTIONS, D), jnp.float32), 0.1, 1.9),
        "key_weight": noise(key_of[2], (SECTIONS, D, KV), 0.1, 0.59765625, ((0, 8),)),
        "key_gain": jnp.clip(1.0 + 0.18 * jax.random.normal(key_of[3], (SECTIONS, HEAD), jnp.float32), 0.1, 1.9),
        "key_cotangent": noise(key_of[4], (SECTIONS, MB, TOKENS, KV), 0.3, 2.0, ((0, 8), (2, 16))),
        "upstream": noise(key_of[5], (MB, TOKENS, D), 0.5, 3.0, ((1, 16),)),
        "master": noise(key_of[6], (SECTIONS, D, KV), 0.1, 0.6, ((0, 8), (1, 16)), jnp.float32),
        "first_moment": noise(key_of[7], (SECTIONS, D, KV), 1.0, 6.0, ((0, 8), (1, 16)), jnp.float32),
        "second_moment": jnp.clip(jnp.exp(math.log(30.0) - 3.4011974 * jax.random.uniform(key_of[8], (SECTIONS, D, KV), jnp.float32) ** block_levels(key_of[8], (SECTIONS, D, KV), ((0, 8), (1, 16)), -0.2, 0.2)), 1.0, 30.0),
    }


beta_one = 0.9
beta_two = 0.95
learn_rate = 0.002
decay_rate = 0.1
adam_eps = 1e-08

def section_backward(inputs):
    acts, gain_row, weight, head_gain, cotan = inputs
    xfloat = acts.astype(jnp.float32).reshape(-1, D)
    inv_rms = lax.rsqrt(lax.optimization_barrier(jnp.mean(xfloat * xfloat, axis=-1, keepdims=True)) + 1e-06)
    normed = (xfloat * inv_rms * gain_row).astype(jnp.bfloat16)
    raw_keys = jnp.dot(normed, weight, preferred_element_type=jnp.float32)
    nrows = raw_keys.shape[0]
    heads = raw_keys.reshape(nrows, HEADS_KV, HEAD)
    head_inv = lax.rsqrt(lax.optimization_barrier(jnp.mean(heads * heads, axis=-1, keepdims=True)) + 1e-06)
    scaled = cotan.astype(jnp.float32).reshape(nrows, HEADS_KV, HEAD) * head_gain
    key_grad = head_inv * (scaled - heads * head_inv * head_inv * lax.optimization_barrier(jnp.mean(scaled * heads, axis=-1, keepdims=True)))
    key_grad = key_grad.reshape(nrows, HEADS_KV * HEAD).astype(jnp.bfloat16)
    weight_grad = lax.dot_general(normed, key_grad, (((0,), (0,)), ((), ())), preferred_element_type=jnp.float32)
    normed_grad = lax.dot_general(key_grad, weight, (((1,), (1,)), ((), ())), preferred_element_type=jnp.float32)
    gated = gain_row * normed_grad
    term = inv_rms * (gated - xfloat * inv_rms * inv_rms * lax.optimization_barrier(jnp.mean(xfloat * gated, axis=-1, keepdims=True)))
    return (term.reshape(acts.shape), weight_grad)

def reference(activations, norm_gain, key_weight, key_gain, key_cotangent, upstream, master, first_moment, second_moment):
    terms, grads = lax.map(section_backward, (activations, norm_gain, key_weight, key_gain, key_cotangent))
    terms = terms.at[-1].add(upstream.astype(jnp.float32))
    input_grad = jnp.flip(jnp.cumsum(jnp.flip(terms, 0), axis=0), 0).astype(jnp.bfloat16)
    new_first = beta_one * first_moment + (1.0 - beta_one) * grads
    new_second = beta_two * second_moment + (1.0 - beta_two) * grads * grads
    corr_one = 1.0 - beta_one ** 10
    corr_two = 1.0 - beta_two ** 10
    update = new_first / corr_one / (jnp.sqrt(new_second / corr_two) + adam_eps) + decay_rate * master
    new_master = master - learn_rate * update
    new_weight = new_master.astype(jnp.bfloat16)
    return (input_grad, new_weight, new_master, new_first, new_second)
```

```python
import jax
import jax.numpy as jnp
from jax import lax
from jax.experimental import pallas as pl
from jax.experimental.pallas import tpu as pltpu
from jax.sharding import PartitionSpec as P

HEAD = 128
HEADS_KV = 4

beta_one = 0.9
beta_two = 0.95
learn_rate = 0.002
decay_rate = 0.1
adam_eps = 1e-08

NX = 4
VMEM_BYTES = 40 * 1024 * 1024


def along_x(k):
    return [(i, (i & 8) | ((((i >> 1) & 3) + k) % NX) * 2 | (i & 1)) for i in range(16)]


SWAP_CORE = [(i, i ^ 1) for i in range(16)]
SWAP_Y = [(i, i ^ 8) for i in range(16)]


def params():
    return pltpu.CompilerParams(vmem_limit_bytes=VMEM_BYTES)


def cost(flops, nbytes):
    return pl.CostEstimate(flops=flops, bytes_accessed=nbytes, transcendentals=0)


def cut_kernel(x_ref, one, two, three, o_one, o_two, o_three):
    o_one[...] = one[...]
    o_two[...] = two[...]
    o_three[...] = three[...]


def cut_columns(acts, xpos):
    rows, width = acts.shape
    blk = width // (2 * NX)

    def spec(k):
        return pl.BlockSpec((rows, blk), lambda y, x: (0, y * NX + lax.rem(x[0] + k, NX)))

    out = jax.ShapeDtypeStruct((rows, 2 * blk), acts.dtype)
    return pl.pallas_call(
        cut_kernel,
        grid_spec=pltpu.PrefetchScalarGridSpec(
            num_scalar_prefetch=1,
            grid=(2,),
            in_specs=[spec(1), spec(2), spec(3)],
            out_specs=[pl.BlockSpec((rows, blk), lambda y, x: (0, y))] * 3,
        ),
        out_shape=[out] * 3,
        compiler_params=params(),
        cost_estimate=cost(0, 12 * rows * blk * 2),
        name="cut_columns",
    )(xpos, acts, acts, acts)


def keys_kernel(steps, width, x_ref, gain_ref, w_ref, hgain_ref, cot_ref, kg_ref, kgs_ref, inv_ref, coef_ref, acc, ssq):
    step = pl.program_id(0)
    xf = x_ref[...].astype(jnp.float32)
    part = jnp.dot(
        (xf * gain_ref[...]).astype(jnp.bfloat16), w_ref[...], preferred_element_type=jnp.float32
    )
    sq = jnp.sum(xf * xf, axis=-1, keepdims=True)

    @pl.when(step == 0)
    def _():
        acc[...] = part
        ssq[...] = jnp.broadcast_to(sq, ssq.shape)

    @pl.when(step > 0)
    def _():
        acc[...] += part
        ssq[...] += sq

    @pl.when(step == steps - 1)
    def _():
        inv = lax.rsqrt(ssq[...] / width + 1e-06)
        hg = hgain_ref[...]
        dots = jnp.zeros_like(inv)
        for h in range(HEADS_KV):
            cols = slice(h * HEAD, (h + 1) * HEAD)
            raw = acc[:, cols] * inv
            hinv = lax.rsqrt(jnp.mean(raw * raw, axis=-1, keepdims=True) + 1e-06)
            scaled = cot_ref[:, cols].astype(jnp.float32) * hg
            kg = hinv * (scaled - raw * hinv * hinv * jnp.mean(scaled * raw, axis=-1, keepdims=True))
            kgs_ref[:, cols] = (kg * inv).astype(jnp.bfloat16)
            kg = kg.astype(jnp.bfloat16)
            kg_ref[:, cols] = kg
            dots += jnp.sum(kg.astype(jnp.float32) * raw, axis=-1, keepdims=True)
        inv_ref[...] = inv
        coef_ref[...] = inv * inv * dots / width


def keys(acts, gain, weight, head_gain, cot):
    rows, width = acts.shape
    kv = weight.shape[1]
    blk = 1280
    steps = width // blk
    return pl.pallas_call(
        lambda *refs: keys_kernel(steps, width, *refs),
        grid=(steps,),
        in_specs=[
            pl.BlockSpec((rows, blk), lambda i: (0, i)),
            pl.BlockSpec((1, blk), lambda i: (0, i)),
            pl.BlockSpec((blk, kv), lambda i: (i, 0)),
            pl.BlockSpec((1, HEAD), lambda i: (0, 0)),
            pl.BlockSpec((rows, kv), lambda i: (0, 0)),
        ],
        out_specs=[
            pl.BlockSpec((rows, kv), lambda i: (0, 0)),
            pl.BlockSpec((rows, kv), lambda i: (0, 0)),
            pl.BlockSpec((rows, HEAD), lambda i: (0, 0)),
            pl.BlockSpec((rows, HEAD), lambda i: (0, 0)),
        ],
        out_shape=[
            jax.ShapeDtypeStruct((rows, kv), jnp.bfloat16),
            jax.ShapeDtypeStruct((rows, kv), jnp.bfloat16),
            jax.ShapeDtypeStruct((rows, HEAD), jnp.float32),
            jax.ShapeDtypeStruct((rows, HEAD), jnp.float32),
        ],
        scratch_shapes=[pltpu.VMEM((rows, kv), jnp.float32), pltpu.VMEM((rows, HEAD), jnp.float32)],
        compiler_params=params(),
        cost_estimate=cost(2 * rows * width * kv, 2 * width * (rows + kv)),
        name="keys",
    )(acts, gain, weight, head_gain, cot)


def term_kernel(kg_ref, w_ref, gain_ref, x_ref, inv_ref, coef_ref, out_ref):
    back = lax.dot_general(
        kg_ref[...], w_ref[...], (((1,), (1,)), ((), ())), preferred_element_type=jnp.float32
    )
    inv = inv_ref[:, :1]
    coef = coef_ref[:, :1]
    term = inv * (gain_ref[...] * back) - coef * x_ref[...].astype(jnp.float32)
    out_ref[0] = term.astype(jnp.bfloat16)


def terms(kg, weight, gain, acts, inv, coef, parts):
    rows, width = acts.shape
    kv = weight.shape[1]
    blk = width // parts
    return pl.pallas_call(
        term_kernel,
        grid=(parts,),
        in_specs=[
            pl.BlockSpec((rows, kv), lambda i: (0, 0)),
            pl.BlockSpec((blk, kv), lambda i: (i, 0)),
            pl.BlockSpec((1, blk), lambda i: (0, i)),
            pl.BlockSpec((rows, blk), lambda i: (0, i)),
            pl.BlockSpec((rows, HEAD), lambda i: (0, 0)),
            pl.BlockSpec((rows, HEAD), lambda i: (0, 0)),
        ],
        out_specs=pl.BlockSpec((1, rows, blk), lambda i: (i, 0, 0)),
        out_shape=jax.ShapeDtypeStruct((parts, rows, blk), jnp.bfloat16),
        compiler_params=params(),
        cost_estimate=cost(2 * rows * width * kv, 2 * width * (2 * rows + kv)),
        name="terms",
    )(kg, weight, gain, acts, inv, coef)


def suffix_kernel(sec_ref, t_ref, up_ref, out_ref):
    total = up_ref[...].astype(jnp.float32)
    for s in reversed(range(t_ref.shape[0])):
        total = total + t_ref[s].astype(jnp.float32)
        out_ref[s] = total.astype(jnp.bfloat16)


def suffix_sums(got, upstream, sec):
    parts, rows, blk = got.shape
    tile = 48
    return pl.pallas_call(
        suffix_kernel,
        grid_spec=pltpu.PrefetchScalarGridSpec(
            num_scalar_prefetch=1,
            grid=(rows // tile,),
            in_specs=[
                pl.BlockSpec((parts, tile, blk), lambda i, s: (0, i, 0)),
                pl.BlockSpec((tile, blk), lambda i, s: (i, s[0])),
            ],
            out_specs=pl.BlockSpec((parts, tile, blk), lambda i, s: (0, i, 0)),
        ),
        out_shape=jax.ShapeDtypeStruct(got.shape, jnp.bfloat16),
        compiler_params=params(),
        cost_estimate=cost(parts * rows * blk, 4 * parts * rows * blk),
        name="suffix_sums",
    )(sec, got, upstream)


def lay_kernel(in_ref, out_ref):
    out_ref[...] = in_ref[0]


def side_by_side(got):
    parts, rows, blk = got.shape
    return pl.pallas_call(
        lay_kernel,
        grid=(parts,),
        in_specs=[pl.BlockSpec((1, rows, blk), lambda i: (i, 0, 0))],
        out_specs=pl.BlockSpec((rows, blk), lambda i: (0, i)),
        out_shape=jax.ShapeDtypeStruct((rows, parts * blk), got.dtype),
        compiler_params=params(),
        cost_estimate=cost(0, 4 * parts * rows * blk),
        name="side_by_side",
    )(got)


def wgrad_kernel(pos_ref, a0, a1, a2, a3, k0, k1, k2, k3, keep_ref, send_ref, full):
    total = None
    for a, k in ((a0, k0), (a1, k1), (a2, k2), (a3, k3)):
        part = lax.dot_general(
            a[...], k[...], (((0,), (0,)), ((), ())), preferred_element_type=jnp.float32
        )
        total = part if total is None else total + part
    full[...] = total
    half = keep_ref.shape[1]
    core = pos_ref[1]
    keep_ref[0] = full[pl.ds(pl.multiple_of(core * half, half), half), :]
    other = pl.multiple_of((1 - core) * half, half)
    send_ref[0] = full[pl.ds(other, half), :].astype(jnp.bfloat16)


def wgrad(acts, got, kgs, got_kgs, pos):
    rows, width = acts.shape
    blk = width // (2 * NX)
    kv = kgs.shape[1]
    half = blk // 2
    got_spec = pl.BlockSpec((rows, blk), lambda y, p: (0, y))
    kgs_spec = pl.BlockSpec((rows, kv), lambda y, p: (0, 0))
    out_spec = pl.BlockSpec((1, half, kv), lambda y, p: (y, 0, 0))
    return pl.pallas_call(
        wgrad_kernel,
        grid_spec=pltpu.PrefetchScalarGridSpec(
            num_scalar_prefetch=1,
            grid=(2,),
            in_specs=[pl.BlockSpec((rows, blk), lambda y, p: (0, y * NX + p[0]))]
            + [got_spec] * 3
            + [kgs_spec] * 4,
            out_specs=[out_spec, out_spec],
            scratch_shapes=[pltpu.VMEM((blk, kv), jnp.float32)],
        ),
        out_shape=[
            jax.ShapeDtypeStruct((2, half, kv), jnp.float32),
            jax.ShapeDtypeStruct((2, half, kv), jnp.bfloat16),
        ],
        compiler_params=params(),
        cost_estimate=cost(2 * 4 * rows * 2 * blk * kv, 2 * 4 * rows * (2 * blk + kv)),
        name="wgrad",
    )(pos, acts, *got, kgs, *got_kgs)


def place_kernel(plan, base_ref, *refs):
    ins, out, sems = refs[:-2], refs[-2], refs[-1]
    copies = []
    for n, (which, index, rows, slot, shift) in enumerate(plan):
        src = ins[which] if index is None else ins[which].at[index]
        at = pl.multiple_of(base_ref[slot] + shift, 32)
        copies.append(pltpu.make_async_copy(src, out.at[pl.ds(at, rows)], sems.at[n]))
    for one in copies:
        one.start()
    for one in copies:
        one.wait()


def place(plan, bases, blocks, rows, kv):
    return pl.pallas_call(
        lambda *refs: place_kernel(plan, *refs),
        in_specs=[pl.BlockSpec(memory_space=pltpu.SMEM)]
        + [pl.BlockSpec(memory_space=pltpu.VMEM)] * len(blocks),
        out_specs=pl.BlockSpec(memory_space=pl.ANY),
        out_shape=jax.ShapeDtypeStruct((rows, kv), jnp.bfloat16),
        scratch_shapes=[pltpu.SemaphoreType.DMA((len(plan),))],
        compiler_params=params(),
        cost_estimate=cost(0, 4 * rows * kv),
        name="place",
    )(bases, *blocks)


def gather_rows(own, y, x, core):
    rows, kv = own.shape
    half = rows // 2
    send = lambda block, perm: lax.ppermute(block, "dp", perm)
    up, down = along_x(1), along_x(-1)
    yr = send(own, SWAP_Y)
    a = send(own, up)
    b = send(own, down)
    c1 = send(jnp.stack([own, a, b]), SWAP_CORE)
    a2 = send(yr, up)
    b2 = send(yr, down)
    f = send(a[:half], up)
    g = send(b[half:], down)
    c2 = send(jnp.stack([yr, a2, b2]), SWAP_CORE)
    f2 = send(a2[:half], up)
    g2 = send(b2[half:], down)
    c3 = send(jnp.stack([f, g, f2, g2]), SWAP_CORE)
    blocks = [own, a, b, yr, a2, b2, f, g, f2, g2, c1, c2, c3]

    def slot(dy, dx, dc):
        return (dy * 3 + dx) * 2 + dc

    table = []
    for dy in range(2):
        for dx in (0, -1, 1, 2):
            for dc in range(2):
                yy = y if dy == 0 else 1 - y
                cc = core if dc == 0 else 1 - core
                table.append((yy * 8 + lax.rem(x + dx + NX, NX) * 2 + cc) * rows)
    bases = jnp.stack(table).astype(jnp.int32)
    at = {(dy, dx, dc): (dy * 4 + i) * 2 + dc for dy in range(2) for i, dx in enumerate((0, -1, 1, 2)) for dc in range(2)}
    plan = []
    for n, (dy, dx) in enumerate(((0, 0), (0, -1), (0, 1), (1, 0), (1, -1), (1, 1))):
        plan.append((n, None, rows, at[dy, dx, 0], 0))
    for n, (dy, shift) in enumerate(((0, 0), (0, half), (1, 0), (1, half))):
        plan.append((6 + n, None, half, at[dy, 2, 0], shift))
    for dy in range(2):
        for i, dx in enumerate((0, -1, 1)):
            plan.append((10 + dy, i, rows, at[dy, dx, 1], 0))
    for n, (dy, shift) in enumerate(((0, 0), (0, half), (1, 0), (1, half))):
        plan.append((12, n, half, at[dy, 2, 1], shift))
    return place(plan, bases, blocks, 16 * rows, kv)


def body(
    activations,
    norm_gain,
    key_weight,
    key_gain,
    key_cotangent,
    upstream,
    master,
    first_moment,
    second_moment,
):
    sections = lax.axis_size("section")
    micro, tok, width = activations.shape[1:]
    rows = micro * tok
    acts = activations.reshape(rows, width)
    weight = key_weight[0]
    kv = weight.shape[1]
    me = lax.axis_index("dp")
    y, x, core = me // 8, lax.rem(me // 2, NX), lax.rem(me, 2)
    pos = jnp.stack([x, core]).astype(jnp.int32)
    sec = lax.axis_index("section").astype(jnp.int32)[None]

    cut = cut_columns(acts, pos)
    got = [lax.ppermute(cut[k - 1], "dp", along_x(k)) for k in (1, 2, 3)]
    kg, kgs, inv, coef = keys(acts, norm_gain, weight, key_gain, key_cotangent.reshape(rows, kv))
    term = terms(kg, weight, norm_gain, acts, inv, coef, sections)
    kgs_late, _ = lax.optimization_barrier((kgs, term))
    got_kgs = [lax.ppermute(kgs_late if k == 2 else kgs, "dp", along_x(k)) for k in (1, 2, 3)]
    theirs = lax.all_to_all(term, "section", 0, 0)
    sums = suffix_sums(theirs, upstream.reshape(rows, width), sec)
    mine = lax.all_to_all(sums, "section", 0, 0)
    input_grad = side_by_side(mine).reshape(activations.shape)

    keep, away = wgrad(acts, got, kgs, got_kgs, pos)
    both = keep + lax.ppermute(away, "dp", SWAP_CORE).astype(jnp.float32)
    here = lax.dynamic_index_in_dim(both, y, 0, keepdims=False)
    there = lax.dynamic_index_in_dim(both, 1 - y, 0, keepdims=False).astype(jnp.bfloat16)
    part = here + lax.ppermute(there, "dp", SWAP_Y).astype(jnp.float32)
    own_rows = part.shape[0]
    gain_rows = lax.dynamic_slice(norm_gain[0], (me * own_rows,), (own_rows,))
    weight_grad = part * gain_rows[:, None]

    master_rows = master[0]
    new_first = beta_one * first_moment[0] + (1.0 - beta_one) * weight_grad
    new_second = beta_two * second_moment[0] + (1.0 - beta_two) * weight_grad * weight_grad
    corr_one = 1.0 - beta_one**10
    corr_two = 1.0 - beta_two**10
    update = (
        new_first / corr_one / (jnp.sqrt(new_second / corr_two) + adam_eps)
        + decay_rate * master_rows
    )
    new_master = master_rows - learn_rate * update
    new_weight = gather_rows(new_master.astype(jnp.bfloat16), y, x, core)
    return (input_grad, new_weight[None], new_master[None], new_first[None], new_second[None])


def solution(mesh):
    return jax.shard_map(
        body,
        mesh=mesh,
        in_specs=(
            P("section", None, "dp", None),
            P("section", None),
            P("section", None, None),
            P("section", None),
            P("section", None, "dp", None),
            P(None, "dp", None),
            P("section", "dp", None),
            P("section", "dp", None),
            P("section", "dp", None),
        ),
        out_specs=(
            P("section", None, "dp", None),
            P("section", None, None),
            P("section", "dp", None),
            P("section", "dp", None),
            P("section", "dp", None),
        ),
        check_vma=False,
    )
```

```python
import jax
import jax.numpy as jnp
from jax import lax
from jax.experimental import pallas as pl
from jax.experimental.pallas import tpu as pltpu
from jax.sharding import PartitionSpec as P

HEAD = 128
HEADS_KV = 4

beta_one = 0.9
beta_two = 0.95
learn_rate = 0.002
decay_rate = 0.1
adam_eps = 1e-08

NX = 4


def along_x(k):
    return [(i, (i & 8) | ((((i >> 1) & 3) + k) % NX) * 2 | (i & 1)) for i in range(16)]


SWAP_CORE = [(i, i ^ 1) for i in range(16)]
SWAP_Y = [(i, i ^ 8) for i in range(16)]

NZ = 4
RINGS_Z = [[0, 1, 2, 3], [4, 5, 6, 7]]
DOWN_Y = [(NZ + z, z) for z in range(NZ)]


def params(mib):
    return pltpu.CompilerParams(vmem_limit_bytes=mib * 1024 * 1024)


def cost(flops, nbytes):
    return pl.CostEstimate(flops=0, bytes_accessed=1, transcendentals=0)


def chip_columns(blk, k):
    x = lax.rem(lax.axis_index("dp") // 2 + k, NX)
    return [pl.ds(pl.multiple_of((y * NX + x) * blk, HEAD), blk) for y in range(2)]


def run_copies(moves, sems):
    copies = [pltpu.make_async_copy(src, dst, sems.at[n]) for n, (src, dst) in enumerate(moves)]
    for one in copies:
        one.start()
    for one in copies:
        one.wait()


def cut_kernel(x_hbm, up, down, far, sems):
    blk = up.shape[1] // 2
    moves = []
    for out, k in ((up, 1), (down, NX - 1), (far, 2)):
        for y, cols in enumerate(chip_columns(blk, k)):
            moves.append((x_hbm.at[:, cols], out.at[:, pl.ds(y * blk, blk)]))
    run_copies(moves, sems)


def cut_columns(acts):
    rows, width = acts.shape
    out = jax.ShapeDtypeStruct((rows, width // NX), acts.dtype)
    return pl.pallas_call(
        cut_kernel,
        in_specs=[pl.BlockSpec(memory_space=pl.ANY)],
        out_specs=[pl.BlockSpec(memory_space=pltpu.VMEM)] * 3,
        out_shape=[out] * 3,
        scratch_shapes=[pltpu.SemaphoreType.DMA((6,))],
        compiler_params=params(60),
        cost_estimate=cost(0, 12 * rows * width // NX),
        name="cut_columns",
    )(acts)


def front_kernel(parts, x_hbm, w_hbm, gain_ref, hgain_ref, cot_ref, after_ref, kgs_ref, term_hbm, xv, wv, tv, acc, kgv, in_sems, out_sems):
    rows, width = xv.shape
    blk = width // parts
    spans = [pl.ds(c * blk, blk) for c in range(parts)]
    loads = []
    for c, span in enumerate(spans):
        loads.append(
            (
                pltpu.make_async_copy(x_hbm.at[:, span], xv.at[:, span], in_sems.at[2 * c]),
                pltpu.make_async_copy(w_hbm.at[span], wv.at[span], in_sems.at[2 * c + 1]),
            )
        )
    for pair in loads:
        for one in pair:
            one.start()
    ssq = None
    for c, span in enumerate(spans):
        for one in loads[c]:
            one.wait()
        xf = xv[:, span].astype(jnp.float32)
        scaled = (xf * gain_ref[:, span]).astype(jnp.bfloat16)
        part = jnp.dot(scaled, wv[span, :], preferred_element_type=jnp.float32)
        sq = jnp.sum(xf * xf, axis=-1, keepdims=True)
        if c == 0:
            acc[...] = part
            ssq = sq
        else:
            acc[...] += part
            ssq = ssq + sq
    inv = lax.rsqrt(ssq / width + 1e-06)
    hg = hgain_ref[...]
    dots = jnp.zeros_like(inv)
    for h in range(HEADS_KV):
        cols = slice(h * HEAD, (h + 1) * HEAD)
        raw = acc[:, cols] * inv
        hinv = lax.rsqrt(jnp.mean(raw * raw, axis=-1, keepdims=True) + 1e-06)
        scaled = cot_ref[:, cols].astype(jnp.float32) * hg
        kg = hinv * (scaled - raw * hinv * hinv * jnp.mean(scaled * raw, axis=-1, keepdims=True))
        kgs_ref[:, cols] = (kg * inv).astype(jnp.bfloat16)
        kg = kg.astype(jnp.bfloat16)
        kgv[:, cols] = kg
        dots += jnp.sum(kg.astype(jnp.float32) * raw, axis=-1, keepdims=True)
    coef = inv * inv * dots / width
    stores = []
    for c, span in enumerate(spans):
        back = lax.dot_general(
            kgv[...], wv[span, :], (((1,), (1,)), ((), ())), preferred_element_type=jnp.float32
        )
        term = inv * (gain_ref[:, span] * back) - coef * xv[:, span].astype(jnp.float32)
        tv[c] = term.astype(jnp.bfloat16)
        stores.append(pltpu.make_async_copy(tv.at[c], term_hbm.at[c], out_sems.at[c]))
        stores[c].start()
    for one in stores:
        one.wait()


def front(acts, gain, weight, head_gain, cot, parts, after):
    rows, width = acts.shape
    kv = weight.shape[1]
    blk = width // parts
    anywhere = pl.BlockSpec(memory_space=pl.ANY)
    inside = pl.BlockSpec(memory_space=pltpu.VMEM)
    return pl.pallas_call(
        lambda *refs: front_kernel(parts, *refs),
        in_specs=[anywhere, anywhere, inside, inside, inside, anywhere],
        out_specs=[inside, anywhere],
        out_shape=[
            jax.ShapeDtypeStruct((rows, kv), jnp.bfloat16),
            jax.ShapeDtypeStruct((parts, rows, blk), jnp.bfloat16),
        ],
        scratch_shapes=[
            pltpu.VMEM((rows, width), jnp.bfloat16),
            pltpu.VMEM((width, kv), jnp.bfloat16),
            pltpu.VMEM((parts, rows, blk), jnp.bfloat16),
            pltpu.VMEM((rows, kv), jnp.float32),
            pltpu.VMEM((rows, kv), jnp.bfloat16),
            pltpu.SemaphoreType.DMA((2 * parts,)),
            pltpu.SemaphoreType.DMA((parts,)),
        ],
        compiler_params=params(60),
        cost_estimate=cost(40 * rows * width * kv, 2 * width * (2 * rows + kv)),
        name="front",
    )(acts, weight, gain, head_gain, cot, after)


def total_kernel(z_ref, t_ref, up_ref, after_ref, out_ref):
    total = up_ref[...].astype(jnp.float32)
    for s in range(t_ref.shape[0]):
        total = total + t_ref[s].astype(jnp.float32)
    out_ref[...] = total.astype(jnp.bfloat16)


def half_total(got, upstream, z, after):
    parts, rows, blk = got.shape
    tile = 96
    return pl.pallas_call(
        total_kernel,
        grid_spec=pltpu.PrefetchScalarGridSpec(
            num_scalar_prefetch=1,
            grid=(rows // tile,),
            in_specs=[
                pl.BlockSpec((parts, tile, blk), lambda i, z: (0, i, 0)),
                pl.BlockSpec((tile, blk), lambda i, z: (i, z[0])),
                pl.BlockSpec(memory_space=pl.ANY),
            ],
            out_specs=pl.BlockSpec((tile, blk), lambda i, z: (i, 0)),
        ),
        out_shape=jax.ShapeDtypeStruct((rows, blk), jnp.bfloat16),
        compiler_params=params(16),
        cost_estimate=cost(parts * rows * blk, 2 * parts * rows * blk),
        name="half_total",
    )(z, got, upstream, after)


def suffix_kernel(z_ref, t_ref, up_ref, above_ref, after_ref, out_ref):
    upper = z_ref[1] == 1
    base = jnp.where(upper, up_ref[...].astype(jnp.float32), above_ref[...].astype(jnp.float32))
    total = base
    for s in reversed(range(t_ref.shape[0])):
        total = total + t_ref[s].astype(jnp.float32)
        out_ref[s] = total.astype(jnp.bfloat16)


def suffix_sums(got, upstream, above, z, after):
    parts, rows, blk = got.shape
    tile = 96
    return pl.pallas_call(
        suffix_kernel,
        grid_spec=pltpu.PrefetchScalarGridSpec(
            num_scalar_prefetch=1,
            grid=(rows // tile,),
            in_specs=[
                pl.BlockSpec((parts, tile, blk), lambda i, z: (0, i, 0)),
                pl.BlockSpec((tile, blk), lambda i, z: (i, z[0])),
                pl.BlockSpec((tile, blk), lambda i, z: (i, 0)),
                pl.BlockSpec(memory_space=pl.ANY),
            ],
            out_specs=pl.BlockSpec((parts, tile, blk), lambda i, z: (0, i, 0)),
        ),
        out_shape=jax.ShapeDtypeStruct(got.shape, jnp.bfloat16),
        compiler_params=params(16),
        cost_estimate=cost(parts * rows * blk, 4 * parts * rows * blk),
        name="suffix_sums",
    )(z, got, upstream, above, after)


def lay_kernel(in_ref, out_ref):
    out_ref[...] = in_ref[0]


def side_by_side(got):
    parts, rows, blk = got.shape
    return pl.pallas_call(
        lay_kernel,
        grid=(parts,),
        in_specs=[pl.BlockSpec((1, rows, blk), lambda i: (i, 0, 0))],
        out_specs=pl.BlockSpec((rows, blk), lambda i: (0, i)),
        out_shape=jax.ShapeDtypeStruct((rows, parts * blk), got.dtype),
        compiler_params=params(16),
        cost_estimate=cost(0, 4 * parts * rows * blk),
        name="side_by_side",
    )(got)


def wgrad_kernel(x_hbm, up, down, far, k0, k1, k3, k2, keep_ref, send_ref, av, kv, full, sems):
    rows, wide = up.shape
    blk = wide // 2
    cols = chip_columns(blk, 0)
    moves = [
        (x_hbm.at[:, cols[0]], av.at[pl.ds(0, rows), pl.ds(0, blk)]),
        (x_hbm.at[:, cols[1]], av.at[pl.ds(0, rows), pl.ds(blk, blk)]),
        (up, av.at[pl.ds(rows, rows)]),
        (down, av.at[pl.ds(2 * rows, rows)]),
        (far, av.at[pl.ds(3 * rows, rows)]),
        (k0, kv.at[pl.ds(0, rows)]),
        (k1, kv.at[pl.ds(rows, rows)]),
        (k3, kv.at[pl.ds(2 * rows, rows)]),
        (k2, kv.at[pl.ds(3 * rows, rows)]),
    ]
    run_copies(moves, sems)
    half = keep_ref.shape[1]
    core = lax.rem(lax.axis_index("dp"), 2)
    own = pl.multiple_of(core * half, half)
    other = pl.multiple_of((1 - core) * half, half)
    for y in range(2):
        full[...] = lax.dot_general(
            av[:, y * blk : (y + 1) * blk], kv[...], (((0,), (0,)), ((), ())), preferred_element_type=jnp.float32
        )
        keep_ref[y] = full[pl.ds(own, half), :]
        send_ref[y] = full[pl.ds(other, half), :].astype(jnp.bfloat16)


def wgrad(acts, got, kgs, got_kgs):
    rows, width = acts.shape
    blk = width // (2 * NX)
    kv = kgs.shape[1]
    half = blk // 2
    anywhere = pl.BlockSpec(memory_space=pl.ANY)
    inside = pl.BlockSpec(memory_space=pltpu.VMEM)
    return pl.pallas_call(
        wgrad_kernel,
        in_specs=[anywhere] * 8,
        out_specs=[inside, inside],
        scratch_shapes=[
            pltpu.VMEM((4 * rows, 2 * blk), jnp.bfloat16),
            pltpu.VMEM((4 * rows, kv), jnp.bfloat16),
            pltpu.VMEM((blk, kv), jnp.float32),
            pltpu.SemaphoreType.DMA((9,)),
        ],
        out_shape=[
            jax.ShapeDtypeStruct((2, half, kv), jnp.float32),
            jax.ShapeDtypeStruct((2, half, kv), jnp.bfloat16),
        ],
        compiler_params=params(58),
        cost_estimate=cost(2 * 4 * rows * 2 * blk * kv, 2 * 4 * rows * (2 * blk + kv)),
        name="wgrad",
    )(acts, *got, kgs, *got_kgs)


def merge_kernel(keep, got, here_ref, there_ref):
    y = lax.axis_index("dp") // 8
    here_ref[...] = keep[y] + got[y].astype(jnp.float32)
    there_ref[...] = (keep[1 - y] + got[1 - y].astype(jnp.float32)).astype(jnp.bfloat16)


def merge(keep, got):
    two, half, kv = keep.shape
    inside = pl.BlockSpec(memory_space=pltpu.VMEM)
    return pl.pallas_call(
        merge_kernel,
        in_specs=[inside, inside],
        out_shape=[
            jax.ShapeDtypeStruct((half, kv), jnp.float32),
            jax.ShapeDtypeStruct((half, kv), jnp.bfloat16),
        ],
        compiler_params=params(16),
        cost_estimate=cost(2 * half * kv, 18 * half * kv),
        name="merge",
    )(keep, got)


def adam_kernel(here, got, gain, master, first, second, o_master, o_first, o_second, o_weight):
    grad = gain[...] * (here[...] + got[...].astype(jnp.float32))
    new_first = beta_one * first[0] + (1.0 - beta_one) * grad
    new_second = beta_two * second[0] + (1.0 - beta_two) * grad * grad
    corr_one = 1.0 - beta_one**10
    corr_two = 1.0 - beta_two**10
    update = (
        new_first / corr_one / (jnp.sqrt(new_second / corr_two) + adam_eps)
        + decay_rate * master[0]
    )
    new_master = master[0] - learn_rate * update
    o_master[0] = new_master
    o_first[0] = new_first
    o_second[0] = new_second
    o_weight[...] = new_master.astype(jnp.bfloat16)


def adam(here, got, gain, master, first, second):
    half, kv = here.shape
    tile = half // 2
    flat = pl.BlockSpec((tile, kv), lambda i: (i, 0))
    deep = pl.BlockSpec((1, tile, kv), lambda i: (0, i, 0))
    out = jax.ShapeDtypeStruct(master.shape, jnp.float32)
    return pl.pallas_call(
        adam_kernel,
        grid=(2,),
        in_specs=[flat, flat, pl.BlockSpec((tile, 1), lambda i: (i, 0)), deep, deep, deep],
        out_specs=[deep, deep, deep, flat],
        out_shape=[out, out, out, jax.ShapeDtypeStruct((half, kv), jnp.bfloat16)],
        compiler_params=params(60),
        cost_estimate=cost(20 * half * kv, 32 * half * kv),
        name="adam",
    )(here, got, gain, master, first, second)


def place(plan, bases, blocks, rows, kv, whole, after):
    prior = ([] if whole is None else [whole]) + list(after)
    count = len(blocks)

    def kernel(base_ref, *refs):
        ins, out, sems = refs[:count], refs[-2], refs[-1]
        moves = []
        for which, index, n, slot, shift in plan:
            src = ins[which].at[pl.ds(index, n)]
            at = pl.multiple_of(base_ref[slot] + shift, 32)
            moves.append((src, out.at[pl.ds(at, n)]))
        run_copies(moves, sems)

    return pl.pallas_call(
        kernel,
        in_specs=[pl.BlockSpec(memory_space=pltpu.SMEM)]
        + [pl.BlockSpec(memory_space=pltpu.VMEM)] * count
        + [pl.BlockSpec(memory_space=pl.ANY)] * len(prior),
        out_specs=pl.BlockSpec(memory_space=pl.ANY),
        out_shape=jax.ShapeDtypeStruct((rows, kv), jnp.bfloat16),
        scratch_shapes=[pltpu.SemaphoreType.DMA((len(plan),))],
        input_output_aliases={} if whole is None else {1 + count: 0},
        compiler_params=params(16),
        cost_estimate=cost(0, 4 * kv * sum(p[2] for p in plan)),
        name="place",
    )(bases, *blocks, *prior)


def stack_kernel(*refs):
    moves, at = [], 0
    for ref in refs[:-2]:
        rows = ref.shape[0]
        moves.append((ref, refs[-2].at[pl.ds(at, rows)]))
        at += rows
    run_copies(moves, refs[-1])


def stacked(blocks):
    rows = sum(b.shape[0] for b in blocks)
    return pl.pallas_call(
        stack_kernel,
        in_specs=[pl.BlockSpec(memory_space=pl.ANY)] * len(blocks),
        out_specs=pl.BlockSpec(memory_space=pltpu.VMEM),
        out_shape=jax.ShapeDtypeStruct((rows, blocks[0].shape[1]), blocks[0].dtype),
        scratch_shapes=[pltpu.SemaphoreType.DMA((len(blocks),))],
        compiler_params=params(16),
        cost_estimate=cost(0, 4 * rows * blocks[0].shape[1]),
        name="stacked",
    )(*blocks)


def gather_rows(own, y, x, core, last):
    rows, kv = own.shape
    half = rows // 2
    send = lambda block, perm: lax.ppermute(block, "dp", perm)
    up, down = along_x(1), along_x(-1)
    yr = send(own, SWAP_Y)
    a = send(own, up)
    b = send(own, down)
    a2 = send(yr, up)
    b2 = send(yr, down)
    f = send(a[:half], up)
    g = send(b[half:], down)
    f2 = send(a2[:half], up)
    g2 = send(b2[half:], down)
    order = (0, -1, 1, 2)
    table = []
    for dy in range(2):
        for dx in order:
            for dc in range(2):
                yy = y if dy == 0 else 1 - y
                cc = core if dc == 0 else 1 - core
                table.append((yy * 8 + lax.rem(x + dx + NX, NX) * 2 + cc) * rows)
    bases = jnp.stack(table).astype(jnp.int32)

    def plan_of(entries, dc):
        return [
            (n, block.shape[0], (dy * 4 + order.index(dx)) * 2 + dc, shift)
            for n, (block, dy, dx, shift) in enumerate(entries)
        ]

    def put(entries, swapped, whole, after=()):
        blocks = [e[0] for e in entries]
        plan = [(n, 0, r, slot, shift) for n, r, slot, shift in plan_of(entries, 0)]
        at = 0
        for n, r, slot, shift in plan_of(entries, 1):
            if len(swapped) == 1:
                plan.append((len(blocks), at, r, slot, shift))
                at += r
            else:
                plan.append((len(blocks) + n, 0, r, slot, shift))
        return place(plan, bases, blocks + swapped, 16 * rows, kv, whole, after)

    near = [(own, 0, 0, 0), (a, 0, -1, 0), (b, 0, 1, 0), (yr, 1, 0, 0)]
    whole = put(near, [send(stacked([e[0] for e in near]), SWAP_CORE)], None)
    middle = [(a2, 1, -1, 0), (b2, 1, 1, 0), (f, 0, 2, 0), (g, 0, 2, half)]
    whole = put(middle, [send(e[0], SWAP_CORE) for e in middle], whole, (last,))
    f2, g2, whole = lax.optimization_barrier((f2, g2, whole))
    swapped = send(jnp.concatenate([f2, g2]), SWAP_CORE)
    return put([(f2, 1, 2, 0), (g2, 1, 2, half)], [swapped], whole)


def body(
    activations,
    norm_gain,
    key_weight,
    key_gain,
    key_cotangent,
    upstream,
    master,
    first_moment,
    second_moment,
):
    micro, tok, width = activations.shape[1:]
    rows = micro * tok
    acts = activations.reshape(rows, width)
    weight = key_weight[0]
    kv = weight.shape[1]
    me = lax.axis_index("dp")
    y, x, core = me // 8, lax.rem(me // 2, NX), lax.rem(me, 2)
    section = lax.axis_index("section")
    zpos = jnp.stack([lax.rem(section, NZ), section // NZ]).astype(jnp.int32)
    upstream = upstream.reshape(rows, width)

    cut = cut_columns(acts)
    got = [lax.ppermute(one, "dp", along_x(k)) for one, k in zip(cut, (1, -1, 2))]
    kgs, term = front(acts, norm_gain, weight, key_gain, key_cotangent.reshape(rows, kv), NZ, cut[0])
    got_kgs = [lax.ppermute(kgs, "dp", along_x(1)), lax.ppermute(kgs, "dp", along_x(-1))]
    kgs_late, *got = lax.optimization_barrier((kgs, *got))
    term, got[0], got[1], got[2], *got_kgs = lax.optimization_barrier((term, *got, *got_kgs))
    got_kgs.append(lax.ppermute(kgs_late, "dp", along_x(2)))
    theirs = lax.all_to_all(term, "section", 0, 0, axis_index_groups=RINGS_Z)

    keep, away = wgrad(acts, got, kgs, got_kgs)
    here, there = merge(keep, lax.ppermute(away, "dp", SWAP_CORE))
    ours = half_total(theirs, upstream, zpos, here)

    above = lax.ppermute(ours, "section", DOWN_Y)
    sums = suffix_sums(theirs, upstream, above, zpos, here)
    mine = lax.all_to_all(sums, "section", 0, 0, axis_index_groups=RINGS_Z)
    input_grad = side_by_side(mine).reshape(activations.shape)

    own_rows = here.shape[0]
    gain_rows = lax.dynamic_slice(norm_gain[0], (me * own_rows,), (own_rows,))[:, None]
    new_master, new_first, new_second, own = adam(
        here, lax.ppermute(there, "dp", SWAP_Y), gain_rows, master, first_moment, second_moment
    )
    new_weight = gather_rows(own, y, x, core, input_grad)
    return (input_grad, new_weight[None], new_master, new_first, new_second)


def solution(mesh):
    return jax.shard_map(
        body,
        mesh=mesh,
        in_specs=(
            P("section", None, "dp", None),
            P("section", None),
            P("section", None, None),
            P("section", None),
            P("section", None, "dp", None),
            P(None, "dp", None),
            P("section", "dp", None),
            P("section", "dp", None),
            P("section", "dp", None),
        ),
        out_specs=(
            P("section", None, "dp", None),
            P("section", None, None),
            P("section", "dp", None),
            P("section", "dp", None),
            P("section", "dp", None),
        ),
        check_vma=False,
    )
```

```python
import jax
import jax.numpy as jnp
from jax import lax
from jax.experimental import pallas as pl
from jax.experimental.pallas import tpu as pltpu
from jax.sharding import PartitionSpec as P

HEAD = 128
HEADS_KV = 4

beta_one = 0.9
beta_two = 0.95
learn_rate = 0.002
decay_rate = 0.1
adam_eps = 1e-08

NX = 4
FRONT_CHUNKS = 4


def along_x(k):
    return [(i, (i & 8) | ((((i >> 1) & 3) + k) % NX) * 2 | (i & 1)) for i in range(16)]


SWAP_CORE = [(i, i ^ 1) for i in range(16)]
SWAP_Y = [(i, i ^ 8) for i in range(16)]


def params(mib):
    return pltpu.CompilerParams(vmem_limit_bytes=mib * 1024 * 1024)


def cost(flops, nbytes):
    return pl.CostEstimate(flops=0, bytes_accessed=1, transcendentals=0)


def chip_columns(blk, k):
    x = lax.rem(lax.axis_index("dp") // 2 + k, NX)
    return [pl.ds(pl.multiple_of((y * NX + x) * blk, HEAD), blk) for y in range(2)]


def run_copies(moves, sems):
    copies = [pltpu.make_async_copy(src, dst, sems.at[n]) for n, (src, dst) in enumerate(moves)]
    for one in copies:
        one.start()
    for one in copies:
        one.wait()


def cut_kernel(x_hbm, up, down, far, sems):
    blk = up.shape[1] // 2
    moves = []
    for out, k in ((up, 1), (down, NX - 1), (far, 2)):
        for y, cols in enumerate(chip_columns(blk, k)):
            moves.append((x_hbm.at[:, cols], out.at[:, pl.ds(y * blk, blk)]))
    run_copies(moves, sems)


def cut_columns(acts):
    rows, width = acts.shape
    out = jax.ShapeDtypeStruct((rows, width // NX), acts.dtype)
    return pl.pallas_call(
        cut_kernel,
        in_specs=[pl.BlockSpec(memory_space=pl.ANY)],
        out_specs=[pl.BlockSpec(memory_space=pltpu.VMEM)] * 3,
        out_shape=[out] * 3,
        scratch_shapes=[pltpu.SemaphoreType.DMA((6,))],
        compiler_params=params(60),
        cost_estimate=cost(0, 12 * rows * width // NX),
        name="cut_columns",
    )(acts)


def front_kernel(parts, x_hbm, w_hbm, gain_ref, hgain_ref, cot_ref, after_ref, kgs_ref, term_hbm, xv, wv, tv, acc, kgv, in_sems, out_sems):
    rows, width = xv.shape
    step = width // FRONT_CHUNKS
    spans = [pl.ds(c * step, step) for c in range(FRONT_CHUNKS)]
    loads = []
    for c, span in enumerate(spans):
        loads.append(
            (
                pltpu.make_async_copy(x_hbm.at[:, span], xv.at[:, span], in_sems.at[2 * c]),
                pltpu.make_async_copy(w_hbm.at[span], wv.at[span], in_sems.at[2 * c + 1]),
            )
        )
    for pair in loads:
        for one in pair:
            one.start()
    ssq = None
    for c, span in enumerate(spans):
        for one in loads[c]:
            one.wait()
        xf = xv[:, span].astype(jnp.float32)
        scaled = (xf * gain_ref[:, span]).astype(jnp.bfloat16)
        part = jnp.dot(scaled, wv[span, :], preferred_element_type=jnp.float32)
        sq = jnp.sum(xf * xf, axis=-1, keepdims=True)
        if c == 0:
            acc[...] = part
            ssq = sq
        else:
            acc[...] += part
            ssq = ssq + sq
    inv = lax.rsqrt(ssq / width + 1e-06)
    hg = hgain_ref[...]
    dots = jnp.zeros_like(inv)
    for h in range(HEADS_KV):
        cols = slice(h * HEAD, (h + 1) * HEAD)
        raw = acc[:, cols] * inv
        hinv = lax.rsqrt(jnp.mean(raw * raw, axis=-1, keepdims=True) + 1e-06)
        scaled = cot_ref[:, cols].astype(jnp.float32) * hg
        kg = hinv * (scaled - raw * hinv * hinv * jnp.mean(scaled * raw, axis=-1, keepdims=True))
        kgs_ref[:, cols] = (kg * inv).astype(jnp.bfloat16)
        kg = kg.astype(jnp.bfloat16)
        kgv[:, cols] = kg
        dots += jnp.sum(kg.astype(jnp.float32) * raw, axis=-1, keepdims=True)
    coef = inv * inv * dots / width
    stores = []
    blk = width // parts
    for c in range(parts):
        span = pl.ds(c * blk, blk)
        back = lax.dot_general(
            kgv[...], wv[span, :], (((1,), (1,)), ((), ())), preferred_element_type=jnp.float32
        )
        term = inv * (gain_ref[:, span] * back) - coef * xv[:, span].astype(jnp.float32)
        tv[c] = term.astype(jnp.bfloat16)
        stores.append(pltpu.make_async_copy(tv.at[c], term_hbm.at[c], out_sems.at[c]))
        stores[c].start()
    for one in stores:
        one.wait()


def front(acts, gain, weight, head_gain, cot, parts, after):
    rows, width = acts.shape
    kv = weight.shape[1]
    blk = width // parts
    anywhere = pl.BlockSpec(memory_space=pl.ANY)
    inside = pl.BlockSpec(memory_space=pltpu.VMEM)
    return pl.pallas_call(
        lambda *refs: front_kernel(parts, *refs),
        in_specs=[anywhere, anywhere, inside, inside, inside, anywhere],
        out_specs=[inside, anywhere],
        out_shape=[
            jax.ShapeDtypeStruct((rows, kv), jnp.bfloat16),
            jax.ShapeDtypeStruct((parts, rows, blk), jnp.bfloat16),
        ],
        scratch_shapes=[
            pltpu.VMEM((rows, width), jnp.bfloat16),
            pltpu.VMEM((width, kv), jnp.bfloat16),
            pltpu.VMEM((parts, rows, blk), jnp.bfloat16),
            pltpu.VMEM((rows, kv), jnp.float32),
            pltpu.VMEM((rows, kv), jnp.bfloat16),
            pltpu.SemaphoreType.DMA((2 * FRONT_CHUNKS,)),
            pltpu.SemaphoreType.DMA((parts,)),
        ],
        compiler_params=params(60),
        cost_estimate=cost(40 * rows * width * kv, 2 * width * (2 * rows + kv)),
        name="front",
    )(acts, weight, gain, head_gain, cot, after)


def row_chunks(rows, count):
    step = rows // count
    return [pl.ds(c * step, step) for c in range(count)]


def suffix_kernel(chunks, t_hbm, up_hbm, after_ref, out_hbm, tv, uv, ov, in_sems, out_sems):
    parts, rows, blk = tv.shape
    cols = pl.ds(pl.multiple_of(lax.axis_index("section") * blk, HEAD), blk)
    spans = row_chunks(rows, chunks)
    loads, stores = [], []
    for c, span in enumerate(spans):
        loads.append(
            (
                pltpu.make_async_copy(t_hbm.at[:, span], tv.at[:, span], in_sems.at[2 * c]),
                pltpu.make_async_copy(up_hbm.at[span, cols], uv.at[span], in_sems.at[2 * c + 1]),
            )
        )
        for one in loads[c]:
            one.start()
    for c, span in enumerate(spans):
        for one in loads[c]:
            one.wait()
        total = uv[span, :].astype(jnp.float32)
        for s in reversed(range(parts)):
            total = total + tv[s, span, :].astype(jnp.float32)
            ov[s, span, :] = total.astype(jnp.bfloat16)
        stores.append(pltpu.make_async_copy(ov.at[:, span], out_hbm.at[:, span], out_sems.at[c]))
        stores[c].start()
    for one in stores:
        one.wait()


def row_chunks(rows, count):
    step = rows // count
    return [pl.ds(c * step, step) for c in range(count)]


def suffix_sums(got, upstream, after):
    parts, rows, blk = got.shape
    chunks = 4
    anywhere = pl.BlockSpec(memory_space=pl.ANY)
    return pl.pallas_call(
        lambda *refs: suffix_kernel(chunks, *refs),
        in_specs=[anywhere] * 3,
        out_specs=anywhere,
        out_shape=jax.ShapeDtypeStruct(got.shape, jnp.bfloat16),
        scratch_shapes=[
            pltpu.VMEM(got.shape, jnp.bfloat16),
            pltpu.VMEM((rows, blk), jnp.bfloat16),
            pltpu.VMEM(got.shape, jnp.bfloat16),
            pltpu.SemaphoreType.DMA((2 * chunks,)),
            pltpu.SemaphoreType.DMA((chunks,)),
        ],
        compiler_params=params(60),
        cost_estimate=cost(parts * rows * blk, 4 * parts * rows * blk),
        name="suffix_sums",
    )(got, upstream, after)


def lay_kernel(in_ref, out_ref):
    out_ref[...] = in_ref[0]


def side_by_side(got):
    parts, rows, blk = got.shape
    return pl.pallas_call(
        lay_kernel,
        grid=(parts,),
        in_specs=[pl.BlockSpec((1, rows, blk), lambda i: (i, 0, 0))],
        out_specs=pl.BlockSpec((rows, blk), lambda i: (0, i)),
        out_shape=jax.ShapeDtypeStruct((rows, parts * blk), got.dtype),
        compiler_params=params(16),
        cost_estimate=cost(0, 4 * parts * rows * blk),
        name="side_by_side",
    )(got)


def wgrad_kernel(x_hbm, up, down, far, k0, k1, k3, k2, keep_hbm, send_hbm, av, kv, full, low, in_sems, out_sems):
    rows, wide = up.shape
    blk = wide // 2
    half = blk // 2
    loads = []
    for n, k in enumerate((k0, k1, k3, k2)):
        loads.append(pltpu.make_async_copy(k, kv.at[pl.ds(n * rows, rows)], in_sems.at[n]))
        loads[n].start()
    cols = chip_columns(blk, 0)
    parts = []
    for y in range(2):
        span = pl.ds(y * blk, blk)
        srcs = (x_hbm.at[:, cols[y]], up.at[:, span], down.at[:, span], far.at[:, span])
        group = []
        for n, src in enumerate(srcs):
            dst = av.at[pl.ds(n * rows, rows), span]
            group.append(pltpu.make_async_copy(src, dst, in_sems.at[4 + 4 * y + n]))
            group[n].start()
        parts.append(group)
    for one in loads:
        one.wait()
    core = lax.rem(lax.axis_index("dp"), 2)
    own = pl.multiple_of(core * half, half)
    other = pl.multiple_of((1 - core) * half, half)
    stores = []
    for y in range(2):
        for one in parts[y]:
            one.wait()
        full[y] = lax.dot_general(
            av[:, y * blk : (y + 1) * blk], kv[...], (((0,), (0,)), ((), ())), preferred_element_type=jnp.float32
        )
        low[y] = full[y, pl.ds(other, half), :].astype(jnp.bfloat16)
        stores.append(pltpu.make_async_copy(full.at[y, pl.ds(own, half)], keep_hbm.at[y], out_sems.at[2 * y]))
        stores.append(pltpu.make_async_copy(low.at[y], send_hbm.at[y], out_sems.at[2 * y + 1]))
        stores[2 * y].start()
        stores[2 * y + 1].start()
    for one in stores:
        one.wait()


def wgrad(acts, got, kgs, got_kgs):
    rows, width = acts.shape
    blk = width // (2 * NX)
    kv = kgs.shape[1]
    half = blk // 2
    anywhere = pl.BlockSpec(memory_space=pl.ANY)
    return pl.pallas_call(
        wgrad_kernel,
        in_specs=[anywhere] * 8,
        out_specs=[anywhere, anywhere],
        scratch_shapes=[
            pltpu.VMEM((4 * rows, 2 * blk), jnp.bfloat16),
            pltpu.VMEM((4 * rows, kv), jnp.bfloat16),
            pltpu.VMEM((2, blk, kv), jnp.float32),
            pltpu.VMEM((2, half, kv), jnp.bfloat16),
            pltpu.SemaphoreType.DMA((12,)),
            pltpu.SemaphoreType.DMA((4,)),
        ],
        out_shape=[
            jax.ShapeDtypeStruct((2, half, kv), jnp.float32),
            jax.ShapeDtypeStruct((2, half, kv), jnp.bfloat16),
        ],
        compiler_params=params(58),
        cost_estimate=cost(2 * 4 * rows * 2 * blk * kv, 2 * 4 * rows * (2 * blk + kv)),
        name="wgrad",
    )(acts, *got, kgs, *got_kgs)


def merge_kernel(keep, got, here_ref, there_ref):
    y = lax.axis_index("dp") // 8
    here_ref[...] = keep[y] + got[y].astype(jnp.float32)
    there_ref[...] = (keep[1 - y] + got[1 - y].astype(jnp.float32)).astype(jnp.bfloat16)


def merge(keep, got):
    two, half, kv = keep.shape
    inside = pl.BlockSpec(memory_space=pltpu.VMEM)
    return pl.pallas_call(
        merge_kernel,
        in_specs=[inside, inside],
        out_shape=[
            jax.ShapeDtypeStruct((half, kv), jnp.float32),
            jax.ShapeDtypeStruct((half, kv), jnp.bfloat16),
        ],
        compiler_params=params(16),
        cost_estimate=cost(2 * half * kv, 18 * half * kv),
        name="merge",
    )(keep, got)


def adam_kernel(here, got, gain, master, first, second, o_master, o_first, o_second, o_weight):
    grad = gain[...] * (here[...] + got[...].astype(jnp.float32))
    new_first = beta_one * first[0] + (1.0 - beta_one) * grad
    new_second = beta_two * second[0] + (1.0 - beta_two) * grad * grad
    corr_one = 1.0 - beta_one**10
    corr_two = 1.0 - beta_two**10
    update = (
        new_first / corr_one / (jnp.sqrt(new_second / corr_two) + adam_eps)
        + decay_rate * master[0]
    )
    new_master = master[0] - learn_rate * update
    o_master[0] = new_master
    o_first[0] = new_first
    o_second[0] = new_second
    o_weight[...] = new_master.astype(jnp.bfloat16)


def adam(here, got, gain, master, first, second):
    half, kv = here.shape
    tile = half // 2
    flat = pl.BlockSpec((tile, kv), lambda i: (i, 0))
    deep = pl.BlockSpec((1, tile, kv), lambda i: (0, i, 0))
    out = jax.ShapeDtypeStruct(master.shape, jnp.float32)
    return pl.pallas_call(
        adam_kernel,
        grid=(2,),
        in_specs=[flat, flat, pl.BlockSpec((tile, 1), lambda i: (i, 0)), deep, deep, deep],
        out_specs=[deep, deep, deep, flat],
        out_shape=[out, out, out, jax.ShapeDtypeStruct((half, kv), jnp.bfloat16)],
        compiler_params=params(60),
        cost_estimate=cost(20 * half * kv, 32 * half * kv),
        name="adam",
    )(here, got, gain, master, first, second)


def place(plan, bases, blocks, rows, kv, whole):
    prior = [] if whole is None else [whole]
    count = len(blocks)
    block = rows // 16

    def kernel(base_ref, *refs):
        ins, out, sems = refs[:count], refs[-2], refs[-1]
        moves = []
        for which, index, slot in plan:
            at = pl.multiple_of(base_ref[slot], 32)
            moves.append((ins[which].at[pl.ds(index, block)], out.at[pl.ds(at, block)]))
        run_copies(moves, sems)

    return pl.pallas_call(
        kernel,
        in_specs=[pl.BlockSpec(memory_space=pltpu.SMEM)]
        + [pl.BlockSpec(memory_space=pltpu.VMEM)] * count
        + [pl.BlockSpec(memory_space=pl.ANY)] * len(prior),
        out_specs=pl.BlockSpec(memory_space=pl.ANY),
        out_shape=jax.ShapeDtypeStruct((rows, kv), jnp.bfloat16),
        scratch_shapes=[pltpu.SemaphoreType.DMA((len(plan),))],
        input_output_aliases={} if whole is None else {1 + count: 0},
        compiler_params=params(16),
        cost_estimate=cost(0, 4 * kv * len(plan) * block),
        name="place",
    )(bases, *blocks, *prior)


def stack_kernel(*refs):
    moves, at = [], 0
    for ref in refs[:-2]:
        rows = ref.shape[0]
        moves.append((ref, refs[-2].at[pl.ds(at, rows)]))
        at += rows
    run_copies(moves, refs[-1])


def stacked(blocks):
    rows = sum(b.shape[0] for b in blocks)
    return pl.pallas_call(
        stack_kernel,
        in_specs=[pl.BlockSpec(memory_space=pl.ANY)] * len(blocks),
        out_specs=pl.BlockSpec(memory_space=pltpu.VMEM),
        out_shape=jax.ShapeDtypeStruct((rows, blocks[0].shape[1]), blocks[0].dtype),
        scratch_shapes=[pltpu.SemaphoreType.DMA((len(blocks),))],
        compiler_params=params(16),
        cost_estimate=cost(0, 4 * rows * blocks[0].shape[1]),
        name="stacked",
    )(*blocks)


def gather_rows(own, y, x, core):
    rows, kv = own.shape
    send = lambda block, perm: lax.ppermute(block, "dp", perm)
    up, down = along_x(1), along_x(-1)
    yr = send(own, SWAP_Y)
    a = send(own, up)
    b = send(own, down)
    a2 = send(yr, up)
    b2 = send(yr, down)
    e = send(own, along_x(2))
    e2 = send(yr, along_x(2))
    order = (0, -1, 1, 2)
    table = []
    for dy in range(2):
        for dx in order:
            for dc in range(2):
                yy = y if dy == 0 else 1 - y
                cc = core if dc == 0 else 1 - core
                table.append((yy * 8 + lax.rem(x + dx + NX, NX) * 2 + cc) * rows)
    bases = jnp.stack(table).astype(jnp.int32)

    def put(entries, swapped, whole):
        blocks = [one[0] for one in entries]
        plan = []
        for n, (block, dy, dx) in enumerate(entries):
            slot = (dy * 4 + order.index(dx)) * 2
            plan.append((n, 0, slot))
            if len(swapped) == 1:
                plan.append((len(blocks), n * rows, slot + 1))
            else:
                plan.append((len(blocks) + n, 0, slot + 1))
        return place(plan, bases, blocks + swapped, 16 * rows, kv, whole)

    near = [(own, 0, 0), (a, 0, -1), (b, 0, 1), (yr, 1, 0)]
    whole = put(near, [send(stacked([one[0] for one in near]), SWAP_CORE)], None)
    a2, e2 = lax.optimization_barrier((a2, e2))
    middle = [(a2, 1, -1), (b2, 1, 1), (e, 0, 2)]
    whole = put(middle, [send(one[0], SWAP_CORE) for one in middle], whole)
    e2, whole = lax.optimization_barrier((e2, whole))
    return put([(e2, 1, 2)], [send(e2, SWAP_CORE)], whole)


def body(
    activations,
    norm_gain,
    key_weight,
    key_gain,
    key_cotangent,
    upstream,
    master,
    first_moment,
    second_moment,
):
    sections = lax.axis_size("section")
    micro, tok, width = activations.shape[1:]
    rows = micro * tok
    acts = activations.reshape(rows, width)
    weight = key_weight[0]
    kv = weight.shape[1]
    me = lax.axis_index("dp")
    y, x, core = me // 8, lax.rem(me // 2, NX), lax.rem(me, 2)
    upstream = upstream.reshape(rows, width)

    cut = cut_columns(acts)
    got = [lax.ppermute(one, "dp", along_x(k)) for one, k in zip(cut, (1, -1, 2))]
    kgs, term = front(acts, norm_gain, weight, key_gain, key_cotangent.reshape(rows, kv), sections, cut[0])
    got_kgs = [lax.ppermute(kgs, "dp", along_x(1)), lax.ppermute(kgs, "dp", along_x(-1))]
    kgs_late, *got = lax.optimization_barrier((kgs, *got))
    got_kgs.append(lax.ppermute(kgs_late, "dp", along_x(2)))
    theirs = lax.all_to_all(term, "section", 0, 0)

    keep, away = wgrad(acts, got, kgs, got_kgs)
    here, there = merge(keep, lax.ppermute(away, "dp", SWAP_CORE))
    sums = suffix_sums(theirs, upstream, here)
    mine = lax.all_to_all(sums, "section", 0, 0)
    input_grad = side_by_side(mine).reshape(activations.shape)

    own_rows = here.shape[0]
    gain_rows = lax.dynamic_slice(norm_gain[0], (me * own_rows,), (own_rows,))[:, None]
    new_master, new_first, new_second, own = adam(
        here, lax.ppermute(there, "dp", SWAP_Y), gain_rows, master, first_moment, second_moment
    )
    new_weight = gather_rows(own, y, x, core)
    return (input_grad, new_weight[None], new_master, new_first, new_second)


def solution(mesh):
    return jax.shard_map(
        body,
        mesh=mesh,
        in_specs=(
            P("section", None, "dp", None),
            P("section", None),
            P("section", None, None),
            P("section", None),
            P("section", None, "dp", None),
            P(None, "dp", None),
            P("section", "dp", None),
            P("section", "dp", None),
            P("section", "dp", None),
        ),
        out_specs=(
            P("section", None, "dp", None),
            P("section", None, None),
            P("section", "dp", None),
            P("section", "dp", None),
            P("section", "dp", None),
        ),
        check_vma=False,
    )
```

```python
import jax
import jax.numpy as jnp
from jax import lax
from jax.experimental import pallas as pl
from jax.experimental.pallas import tpu as pltpu
from jax.sharding import PartitionSpec as P

HEAD = 128
HEADS_KV = 4

beta_one = 0.9
beta_two = 0.95
learn_rate = 0.002
decay_rate = 0.1
adam_eps = 1e-08

NX = 4
FRONT_CHUNKS = 4


def along_x(k):
    return [(i, (i & 8) | ((((i >> 1) & 3) + k) % NX) * 2 | (i & 1)) for i in range(16)]


SWAP_CORE = [(i, i ^ 1) for i in range(16)]
SWAP_Y = [(i, i ^ 8) for i in range(16)]


def params(mib):
    return pltpu.CompilerParams(vmem_limit_bytes=mib * 1024 * 1024)


def cost(flops, nbytes):
    return pl.CostEstimate(flops=0, bytes_accessed=1, transcendentals=0)


def chip_columns(blk, k):
    x = lax.rem(lax.axis_index("dp") // 2 + k, NX)
    return [pl.ds(pl.multiple_of((y * NX + x) * blk, HEAD), blk) for y in range(2)]


def run_copies(moves, sems):
    copies = [pltpu.make_async_copy(src, dst, sems.at[n]) for n, (src, dst) in enumerate(moves)]
    for one in copies:
        one.start()
    for one in copies:
        one.wait()


def cut_kernel(x_hbm, up, down, far, sems):
    blk = up.shape[1] // 2
    moves = []
    for out, k in ((up, 1), (down, NX - 1), (far, 2)):
        for y, cols in enumerate(chip_columns(blk, k)):
            moves.append((x_hbm.at[:, cols], out.at[:, pl.ds(y * blk, blk)]))
    run_copies(moves, sems)


def cut_columns(acts):
    rows, width = acts.shape
    out = jax.ShapeDtypeStruct((rows, width // NX), acts.dtype)
    return pl.pallas_call(
        cut_kernel,
        in_specs=[pl.BlockSpec(memory_space=pl.ANY)],
        out_specs=[pl.BlockSpec(memory_space=pltpu.VMEM)] * 3,
        out_shape=[out] * 3,
        scratch_shapes=[pltpu.SemaphoreType.DMA((6,))],
        compiler_params=params(60),
        cost_estimate=cost(0, 12 * rows * width // NX),
        name="cut_columns",
    )(acts)


def front_kernel(parts, x_hbm, w_hbm, gain_ref, hgain_ref, cot_ref, after_ref, kgs_ref, term_hbm, xv, wv, tv, acc, kgv, in_sems, out_sems):
    rows, width = xv.shape
    step = width // FRONT_CHUNKS
    spans = [pl.ds(c * step, step) for c in range(FRONT_CHUNKS)]
    loads = []
    for c, span in enumerate(spans):
        loads.append(
            (
                pltpu.make_async_copy(x_hbm.at[:, span], xv.at[:, span], in_sems.at[2 * c]),
                pltpu.make_async_copy(w_hbm.at[span], wv.at[span], in_sems.at[2 * c + 1]),
            )
        )
    for pair in loads:
        for one in pair:
            one.start()
    ssq = None
    for c, span in enumerate(spans):
        for one in loads[c]:
            one.wait()
        xf = xv[:, span].astype(jnp.float32)
        scaled = (xf * gain_ref[:, span]).astype(jnp.bfloat16)
        part = jnp.dot(scaled, wv[span, :], preferred_element_type=jnp.float32)
        sq = jnp.sum(xf * xf, axis=-1, keepdims=True)
        if c == 0:
            acc[...] = part
            ssq = sq
        else:
            acc[...] += part
            ssq = ssq + sq
    inv = lax.rsqrt(ssq / width + 1e-06)
    hg = hgain_ref[...]
    dots = jnp.zeros_like(inv)
    for h in range(HEADS_KV):
        cols = slice(h * HEAD, (h + 1) * HEAD)
        raw = acc[:, cols] * inv
        hinv = lax.rsqrt(jnp.mean(raw * raw, axis=-1, keepdims=True) + 1e-06)
        scaled = cot_ref[:, cols].astype(jnp.float32) * hg
        kg = hinv * (scaled - raw * hinv * hinv * jnp.mean(scaled * raw, axis=-1, keepdims=True))
        kgs_ref[:, cols] = (kg * inv).astype(jnp.bfloat16)
        kg = kg.astype(jnp.bfloat16)
        kgv[:, cols] = kg
        dots += jnp.sum(kg.astype(jnp.float32) * raw, axis=-1, keepdims=True)
    coef = inv * inv * dots / width
    stores = []
    blk = width // parts
    for c in range(parts):
        span = pl.ds(c * blk, blk)
        back = lax.dot_general(
            kgv[...], wv[span, :], (((1,), (1,)), ((), ())), preferred_element_type=jnp.float32
        )
        term = inv * (gain_ref[:, span] * back) - coef * xv[:, span].astype(jnp.float32)
        tv[c] = term.astype(jnp.bfloat16)
        stores.append(pltpu.make_async_copy(tv.at[c], term_hbm.at[c], out_sems.at[c]))
        stores[c].start()
    for one in stores:
        one.wait()


def front(acts, gain, weight, head_gain, cot, parts, after):
    rows, width = acts.shape
    kv = weight.shape[1]
    blk = width // parts
    anywhere = pl.BlockSpec(memory_space=pl.ANY)
    inside = pl.BlockSpec(memory_space=pltpu.VMEM)
    return pl.pallas_call(
        lambda *refs: front_kernel(parts, *refs),
        in_specs=[anywhere, anywhere, inside, inside, inside, anywhere],
        out_specs=[inside, anywhere],
        out_shape=[
            jax.ShapeDtypeStruct((rows, kv), jnp.bfloat16),
            jax.ShapeDtypeStruct((parts, rows, blk), jnp.bfloat16),
        ],
        scratch_shapes=[
            pltpu.VMEM((rows, width), jnp.bfloat16),
            pltpu.VMEM((width, kv), jnp.bfloat16),
            pltpu.VMEM((parts, rows, blk), jnp.bfloat16),
            pltpu.VMEM((rows, kv), jnp.float32),
            pltpu.VMEM((rows, kv), jnp.bfloat16),
            pltpu.SemaphoreType.DMA((2 * FRONT_CHUNKS,)),
            pltpu.SemaphoreType.DMA((parts,)),
        ],
        compiler_params=params(60),
        cost_estimate=cost(40 * rows * width * kv, 2 * width * (2 * rows + kv)),
        name="front",
    )(acts, weight, gain, head_gain, cot, after)


def row_chunks(rows, count):
    step = rows // count
    return [pl.ds(c * step, step) for c in range(count)]


def suffix_kernel(chunks, t_hbm, up_hbm, after_ref, out_hbm, tv, uv, ov, in_sems, out_sems):
    parts, rows, blk = tv.shape
    cols = pl.ds(pl.multiple_of(lax.axis_index("section") * blk, HEAD), blk)
    spans = row_chunks(rows, chunks)
    loads, stores = [], []
    for c, span in enumerate(spans):
        loads.append(
            (
                pltpu.make_async_copy(t_hbm.at[:, span], tv.at[:, span], in_sems.at[2 * c]),
                pltpu.make_async_copy(up_hbm.at[span, cols], uv.at[span], in_sems.at[2 * c + 1]),
            )
        )
        for one in loads[c]:
            one.start()
    for c, span in enumerate(spans):
        for one in loads[c]:
            one.wait()
        total = uv[span, :].astype(jnp.float32)
        for s in reversed(range(parts)):
            total = total + tv[s, span, :].astype(jnp.float32)
            ov[s, span, :] = total.astype(jnp.bfloat16)
        stores.append(pltpu.make_async_copy(ov.at[:, span], out_hbm.at[:, span], out_sems.at[c]))
        stores[c].start()
    for one in stores:
        one.wait()


def row_chunks(rows, count):
    step = rows // count
    return [pl.ds(c * step, step) for c in range(count)]


def suffix_sums(got, upstream, after):
    parts, rows, blk = got.shape
    chunks = 4
    anywhere = pl.BlockSpec(memory_space=pl.ANY)
    return pl.pallas_call(
        lambda *refs: suffix_kernel(chunks, *refs),
        in_specs=[anywhere] * 3,
        out_specs=anywhere,
        out_shape=jax.ShapeDtypeStruct(got.shape, jnp.bfloat16),
        scratch_shapes=[
            pltpu.VMEM(got.shape, jnp.bfloat16),
            pltpu.VMEM((rows, blk), jnp.bfloat16),
            pltpu.VMEM(got.shape, jnp.bfloat16),
            pltpu.SemaphoreType.DMA((2 * chunks,)),
            pltpu.SemaphoreType.DMA((chunks,)),
        ],
        compiler_params=params(60),
        cost_estimate=cost(parts * rows * blk, 4 * parts * rows * blk),
        name="suffix_sums",
    )(got, upstream, after)


def lay_kernel(in_ref, out_ref):
    blk = in_ref.shape[2]
    for p in range(in_ref.shape[0]):
        out_ref[:, p * blk : (p + 1) * blk] = in_ref[p]


def side_by_side(got):
    parts, rows, blk = got.shape
    some = parts // 2
    return pl.pallas_call(
        lay_kernel,
        grid=(2,),
        in_specs=[pl.BlockSpec((some, rows, blk), lambda i: (i, 0, 0))],
        out_specs=pl.BlockSpec((rows, some * blk), lambda i: (0, i)),
        out_shape=jax.ShapeDtypeStruct((rows, parts * blk), got.dtype),
        compiler_params=params(16),
        cost_estimate=cost(0, 4 * parts * rows * blk),
        name="side_by_side",
    )(got)


def wgrad_kernel(x_hbm, up, down, far, k0, k1, k3, k2, keep_hbm, send_hbm, av, kv, full, low, in_sems, out_sems):
    rows, wide = up.shape
    blk = wide // 2
    half = blk // 2
    loads = []
    for n, k in enumerate((k0, k1, k3, k2)):
        loads.append(pltpu.make_async_copy(k, kv.at[pl.ds(n * rows, rows)], in_sems.at[n]))
        loads[n].start()
    cols = chip_columns(blk, 0)
    parts = []
    for y in range(2):
        span = pl.ds(y * blk, blk)
        srcs = (x_hbm.at[:, cols[y]], up.at[:, span], down.at[:, span], far.at[:, span])
        group = []
        for n, src in enumerate(srcs):
            dst = av.at[pl.ds(n * rows, rows), span]
            group.append(pltpu.make_async_copy(src, dst, in_sems.at[4 + 4 * y + n]))
            group[n].start()
        parts.append(group)
    for one in loads:
        one.wait()
    core = lax.rem(lax.axis_index("dp"), 2)
    own = pl.multiple_of(core * half, half)
    other = pl.multiple_of((1 - core) * half, half)
    stores = []
    for y in range(2):
        for one in parts[y]:
            one.wait()
        full[y] = lax.dot_general(
            av[:, y * blk : (y + 1) * blk], kv[...], (((0,), (0,)), ((), ())), preferred_element_type=jnp.float32
        )
        low[y] = full[y, pl.ds(other, half), :].astype(jnp.bfloat16)
        stores.append(pltpu.make_async_copy(full.at[y, pl.ds(own, half)], keep_hbm.at[y], out_sems.at[2 * y]))
        stores.append(pltpu.make_async_copy(low.at[y], send_hbm.at[y], out_sems.at[2 * y + 1]))
        stores[2 * y].start()
        stores[2 * y + 1].start()
    for one in stores:
        one.wait()


def wgrad(acts, got, kgs, got_kgs):
    rows, width = acts.shape
    blk = width // (2 * NX)
    kv = kgs.shape[1]
    half = blk // 2
    anywhere = pl.BlockSpec(memory_space=pl.ANY)
    return pl.pallas_call(
        wgrad_kernel,
        in_specs=[anywhere] * 8,
        out_specs=[anywhere, anywhere],
        scratch_shapes=[
            pltpu.VMEM((4 * rows, 2 * blk), jnp.bfloat16),
            pltpu.VMEM((4 * rows, kv), jnp.bfloat16),
            pltpu.VMEM((2, blk, kv), jnp.float32),
            pltpu.VMEM((2, half, kv), jnp.bfloat16),
            pltpu.SemaphoreType.DMA((12,)),
            pltpu.SemaphoreType.DMA((4,)),
        ],
        out_shape=[
            jax.ShapeDtypeStruct((2, half, kv), jnp.float32),
            jax.ShapeDtypeStruct((2, half, kv), jnp.bfloat16),
        ],
        compiler_params=params(40),
        cost_estimate=cost(2 * 4 * rows * 2 * blk * kv, 2 * 4 * rows * (2 * blk + kv)),
        name="wgrad",
    )(acts, *got, kgs, *got_kgs)


def merge_kernel(keep, got, here_ref, there_ref):
    y = lax.axis_index("dp") // 8
    here_ref[...] = keep[y] + got[y].astype(jnp.float32)
    there_ref[...] = (keep[1 - y] + got[1 - y].astype(jnp.float32)).astype(jnp.bfloat16)


def merge(keep, got):
    two, half, kv = keep.shape
    inside = pl.BlockSpec(memory_space=pltpu.VMEM)
    return pl.pallas_call(
        merge_kernel,
        in_specs=[inside, inside],
        out_shape=[
            jax.ShapeDtypeStruct((half, kv), jnp.float32),
            jax.ShapeDtypeStruct((half, kv), jnp.bfloat16),
        ],
        compiler_params=params(16),
        cost_estimate=cost(2 * half * kv, 18 * half * kv),
        name="merge",
    )(keep, got)


def adam_kernel(here, got, gain, master, first, second, o_master, o_first, o_second, o_weight):
    grad = gain[...] * (here[...] + got[...].astype(jnp.float32))
    new_first = beta_one * first[0] + (1.0 - beta_one) * grad
    new_second = beta_two * second[0] + (1.0 - beta_two) * grad * grad
    corr_one = 1.0 - beta_one**10
    corr_two = 1.0 - beta_two**10
    update = (
        new_first / corr_one / (jnp.sqrt(new_second / corr_two) + adam_eps)
        + decay_rate * master[0]
    )
    new_master = master[0] - learn_rate * update
    o_master[0] = new_master
    o_first[0] = new_first
    o_second[0] = new_second
    o_weight[...] = new_master.astype(jnp.bfloat16)


def adam(here, got, gain, master, first, second):
    half, kv = here.shape
    tile = half // 2
    flat = pl.BlockSpec((tile, kv), lambda i: (i, 0))
    deep = pl.BlockSpec((1, tile, kv), lambda i: (0, i, 0))
    out = jax.ShapeDtypeStruct(master.shape, jnp.float32)
    return pl.pallas_call(
        adam_kernel,
        grid=(2,),
        in_specs=[flat, flat, pl.BlockSpec((tile, 1), lambda i: (i, 0)), deep, deep, deep],
        out_specs=[deep, deep, deep, flat],
        out_shape=[out, out, out, jax.ShapeDtypeStruct((half, kv), jnp.bfloat16)],
        compiler_params=params(16),
        cost_estimate=cost(20 * half * kv, 32 * half * kv),
        name="adam",
    )(here, got, gain, master, first, second)


def place(plan, bases, blocks, rows, kv, whole):
    prior = [] if whole is None else [whole]
    count = len(blocks)
    block = rows // 16

    def kernel(base_ref, *refs):
        ins, out, sems = refs[:count], refs[-2], refs[-1]
        moves = []
        for which, index, slot in plan:
            at = pl.multiple_of(base_ref[slot], 32)
            moves.append((ins[which].at[pl.ds(index, block)], out.at[pl.ds(at, block)]))
        run_copies(moves, sems)

    return pl.pallas_call(
        kernel,
        in_specs=[pl.BlockSpec(memory_space=pltpu.SMEM)]
        + [pl.BlockSpec(memory_space=pltpu.VMEM)] * count
        + [pl.BlockSpec(memory_space=pl.ANY)] * len(prior),
        out_specs=pl.BlockSpec(memory_space=pl.ANY),
        out_shape=jax.ShapeDtypeStruct((rows, kv), jnp.bfloat16),
        scratch_shapes=[pltpu.SemaphoreType.DMA((len(plan),))],
        input_output_aliases={} if whole is None else {1 + count: 0},
        compiler_params=params(16),
        cost_estimate=cost(0, 4 * kv * len(plan) * block),
        name="place",
    )(bases, *blocks, *prior)


def spread(slots, bases, blocks, rows):
    count = len(blocks)
    block, kv = blocks[0].shape

    def kernel(base_ref, *refs):
        ins, (stack, whole, sems) = refs[:count], refs[count:]
        moves = []
        for n, slot in enumerate(slots):
            at = pl.multiple_of(base_ref[slot], 32)
            moves.append((ins[n], stack.at[pl.ds(n * block, block)]))
            moves.append((ins[n], whole.at[pl.ds(at, block)]))
        run_copies(moves, sems)

    return pl.pallas_call(
        kernel,
        in_specs=[pl.BlockSpec(memory_space=pltpu.SMEM)]
        + [pl.BlockSpec(memory_space=pltpu.VMEM)] * count,
        out_specs=[pl.BlockSpec(memory_space=pl.ANY)] * 2,
        out_shape=[
            jax.ShapeDtypeStruct((count * block, kv), jnp.bfloat16),
            jax.ShapeDtypeStruct((rows, kv), jnp.bfloat16),
        ],
        scratch_shapes=[pltpu.SemaphoreType.DMA((2 * count,))],
        compiler_params=params(16),
        cost_estimate=cost(0, 6 * count * block * kv),
        name="spread",
    )(bases, *blocks)


def gather_rows(own, y, x, core):
    rows, kv = own.shape
    send = lambda block, perm: lax.ppermute(block, "dp", perm)
    up, down = along_x(1), along_x(-1)
    yr = send(own, SWAP_Y)
    a = send(own, up)
    b = send(own, down)
    a2 = send(yr, up)
    b2 = send(yr, down)
    e = send(own, along_x(2))
    e2 = send(yr, along_x(2))
    order = (0, -1, 1, 2)
    table = []
    for dy in range(2):
        for dx in order:
            for dc in range(2):
                yy = y if dy == 0 else 1 - y
                cc = core if dc == 0 else 1 - core
                table.append((yy * 8 + lax.rem(x + dx + NX, NX) * 2 + cc) * rows)
    bases = jnp.stack(table).astype(jnp.int32)

    def put(entries, whole, others=()):
        blocks = [one[0] for one in entries]
        plan = []
        for n, (block, dy, dx) in enumerate(entries):
            plan.append((n, 0, (dy * 4 + order.index(dx)) * 2))
        for group, swapped in others:
            for n, (block, dy, dx) in enumerate(group):
                slot = (dy * 4 + order.index(dx)) * 2 + 1
                one = 0 if len(swapped) == 1 else n
                plan.append((len(blocks) + one, (n - one) * rows, slot))
            blocks = blocks + swapped
        return place(plan, bases, blocks, 16 * rows, kv, whole)

    near = [(own, 0, 0), (a, 0, -1), (b, 0, 1), (yr, 1, 0)]
    slots = [(dy * 4 + order.index(dx)) * 2 for _, dy, dx in near]
    stack, whole = spread(slots, bases, [one[0] for one in near], 16 * rows)
    c1 = send(stack, SWAP_CORE)
    a2, e2 = lax.optimization_barrier((a2, e2))
    middle = [(a2, 1, -1), (b2, 1, 1), (e, 0, 2)]
    swapped = [send(one[0], SWAP_CORE) for one in middle]
    whole = put(middle, whole, [(near, [c1]), (middle, swapped)])
    e2, whole = lax.optimization_barrier((e2, whole))
    return put([(e2, 1, 2)], whole, [([(e2, 1, 2)], [send(e2, SWAP_CORE)])])


def body(
    activations,
    norm_gain,
    key_weight,
    key_gain,
    key_cotangent,
    upstream,
    master,
    first_moment,
    second_moment,
):
    sections = lax.axis_size("section")
    micro, tok, width = activations.shape[1:]
    rows = micro * tok
    acts = activations.reshape(rows, width)
    weight = key_weight[0]
    kv = weight.shape[1]
    me = lax.axis_index("dp")
    y, x, core = me // 8, lax.rem(me // 2, NX), lax.rem(me, 2)
    upstream = upstream.reshape(rows, width)

    cut = cut_columns(acts)
    got = [lax.ppermute(one, "dp", along_x(k)) for one, k in zip(cut, (1, -1, 2))]
    kgs, term = front(acts, norm_gain, weight, key_gain, key_cotangent.reshape(rows, kv), sections, cut[0])
    got_kgs = [lax.ppermute(kgs, "dp", along_x(1)), lax.ppermute(kgs, "dp", along_x(-1))]
    kgs_late, *got = lax.optimization_barrier((kgs, *got))
    got_kgs.append(lax.ppermute(kgs_late, "dp", along_x(2)))
    theirs = lax.all_to_all(term, "section", 0, 0)

    keep, away = wgrad(acts, got, kgs, got_kgs)
    here, there = merge(keep, lax.ppermute(away, "dp", SWAP_CORE))
    sums = suffix_sums(theirs, upstream, here)
    mine = lax.all_to_all(sums, "section", 0, 0)
    input_grad = side_by_side(mine).reshape(activations.shape)

    own_rows = here.shape[0]
    gain_rows = lax.dynamic_slice(norm_gain[0], (me * own_rows,), (own_rows,))[:, None]
    new_master, new_first, new_second, own = adam(
        here, lax.ppermute(there, "dp", SWAP_Y), gain_rows, master, first_moment, second_moment
    )
    new_weight = gather_rows(own, y, x, core)
    return (input_grad, new_weight[None], new_master, new_first, new_second)


def solution(mesh):
    return jax.shard_map(
        body,
        mesh=mesh,
        in_specs=(
            P("section", None, "dp", None),
            P("section", None),
            P("section", None, None),
            P("section", None),
            P("section", None, "dp", None),
            P(None, "dp", None),
            P("section", "dp", None),
            P("section", "dp", None),
            P("section", "dp", None),
        ),
        out_specs=(
            P("section", None, "dp", None),
            P("section", None, None),
            P("section", "dp", None),
            P("section", "dp", None),
            P("section", "dp", None),
        ),
        check_vma=False,
    )
```

```python
import jax
import jax.numpy as jnp
from jax import lax
from jax.experimental import pallas as pl
from jax.experimental.pallas import tpu as pltpu
from jax.sharding import PartitionSpec as P

HEAD = 128
HEADS_KV = 4

beta_one = 0.9
beta_two = 0.95
learn_rate = 0.002
decay_rate = 0.1
adam_eps = 1e-08

NX = 4
FRONT_CHUNKS = 4


def along_x(k):
    return [(i, (i & 8) | ((((i >> 1) & 3) + k) % NX) * 2 | (i & 1)) for i in range(16)]


SWAP_CORE = [(i, i ^ 1) for i in range(16)]
SWAP_Y = [(i, i ^ 8) for i in range(16)]


def params(mib):
    return pltpu.CompilerParams(vmem_limit_bytes=mib * 1024 * 1024)


def cost(flops, nbytes):
    return pl.CostEstimate(flops=0, bytes_accessed=1, transcendentals=0)


def chip_columns(blk, k):
    x = lax.rem(lax.axis_index("dp") // 2 + k, NX)
    return [pl.ds(pl.multiple_of((y * NX + x) * blk, HEAD), blk) for y in range(2)]


def run_copies(moves, sems):
    copies = [pltpu.make_async_copy(src, dst, sems.at[n]) for n, (src, dst) in enumerate(moves)]
    for one in copies:
        one.start()
    for one in copies:
        one.wait()


def cut_kernel(x_hbm, up, down, far, sems):
    blk = up.shape[1] // 2
    moves = []
    for out, k in ((up, 1), (down, NX - 1), (far, 2)):
        for y, cols in enumerate(chip_columns(blk, k)):
            moves.append((x_hbm.at[:, cols], out.at[:, pl.ds(y * blk, blk)]))
    run_copies(moves, sems)


def cut_columns(acts):
    rows, width = acts.shape
    out = jax.ShapeDtypeStruct((rows, width // NX), acts.dtype)
    return pl.pallas_call(
        cut_kernel,
        in_specs=[pl.BlockSpec(memory_space=pl.ANY)],
        out_specs=[pl.BlockSpec(memory_space=pltpu.VMEM)] * 3,
        out_shape=[out] * 3,
        scratch_shapes=[pltpu.SemaphoreType.DMA((6,))],
        compiler_params=params(60),
        cost_estimate=cost(0, 12 * rows * width // NX),
        name="cut_columns",
    )(acts)


def front_kernel(parts, x_hbm, w_hbm, gain_ref, hgain_ref, cot_ref, after_ref, kgs_ref, term_hbm, xv, wv, tv, acc, kgv, in_sems, out_sems):
    rows, width = xv.shape
    step = width // FRONT_CHUNKS
    spans = [pl.ds(c * step, step) for c in range(FRONT_CHUNKS)]
    loads = []
    for c, span in enumerate(spans):
        loads.append(
            (
                pltpu.make_async_copy(x_hbm.at[:, span], xv.at[:, span], in_sems.at[2 * c]),
                pltpu.make_async_copy(w_hbm.at[span], wv.at[span], in_sems.at[2 * c + 1]),
            )
        )
    for pair in loads:
        for one in pair:
            one.start()
    ssq = None
    for c, span in enumerate(spans):
        for one in loads[c]:
            one.wait()
        xf = xv[:, span].astype(jnp.float32)
        scaled = (xf * gain_ref[:, span]).astype(jnp.bfloat16)
        part = jnp.dot(scaled, wv[span, :], preferred_element_type=jnp.float32)
        sq = jnp.sum(xf * xf, axis=-1, keepdims=True)
        if c == 0:
            acc[...] = part
            ssq = sq
        else:
            acc[...] += part
            ssq = ssq + sq
    inv = lax.rsqrt(ssq / width + 1e-06)
    hg = hgain_ref[...]
    dots = jnp.zeros_like(inv)
    for h in range(HEADS_KV):
        cols = slice(h * HEAD, (h + 1) * HEAD)
        raw = acc[:, cols] * inv
        hinv = lax.rsqrt(jnp.mean(raw * raw, axis=-1, keepdims=True) + 1e-06)
        scaled = cot_ref[:, cols].astype(jnp.float32) * hg
        kg = hinv * (scaled - raw * hinv * hinv * jnp.mean(scaled * raw, axis=-1, keepdims=True))
        kgs_ref[:, cols] = (kg * inv).astype(jnp.bfloat16)
        kg = kg.astype(jnp.bfloat16)
        kgv[:, cols] = kg
        dots += jnp.sum(kg.astype(jnp.float32) * raw, axis=-1, keepdims=True)
    coef = inv * inv * dots / width
    stores = []
    blk = width // parts
    for c in range(parts):
        span = pl.ds(c * blk, blk)
        back = lax.dot_general(
            kgv[...], wv[span, :], (((1,), (1,)), ((), ())), preferred_element_type=jnp.float32
        )
        term = inv * (gain_ref[:, span] * back) - coef * xv[:, span].astype(jnp.float32)
        tv[c] = term.astype(jnp.bfloat16)
        stores.append(pltpu.make_async_copy(tv.at[c], term_hbm.at[c], out_sems.at[c]))
        stores[c].start()
    for one in stores:
        one.wait()


def front(acts, gain, weight, head_gain, cot, parts, after):
    rows, width = acts.shape
    kv = weight.shape[1]
    blk = width // parts
    anywhere = pl.BlockSpec(memory_space=pl.ANY)
    inside = pl.BlockSpec(memory_space=pltpu.VMEM)
    return pl.pallas_call(
        lambda *refs: front_kernel(parts, *refs),
        in_specs=[anywhere, anywhere, inside, inside, inside, anywhere],
        out_specs=[inside, anywhere],
        out_shape=[
            jax.ShapeDtypeStruct((rows, kv), jnp.bfloat16),
            jax.ShapeDtypeStruct((parts, rows, blk), jnp.bfloat16),
        ],
        scratch_shapes=[
            pltpu.VMEM((rows, width), jnp.bfloat16),
            pltpu.VMEM((width, kv), jnp.bfloat16),
            pltpu.VMEM((parts, rows, blk), jnp.bfloat16),
            pltpu.VMEM((rows, kv), jnp.float32),
            pltpu.VMEM((rows, kv), jnp.bfloat16),
            pltpu.SemaphoreType.DMA((2 * FRONT_CHUNKS,)),
            pltpu.SemaphoreType.DMA((parts,)),
        ],
        compiler_params=params(60),
        cost_estimate=cost(40 * rows * width * kv, 2 * width * (2 * rows + kv)),
        name="front",
    )(acts, weight, gain, head_gain, cot, after)


def row_chunks(rows, count):
    step = rows // count
    return [pl.ds(c * step, step) for c in range(count)]


def suffix_kernel(chunks, t_hbm, up_hbm, after_ref, out_hbm, tv, uv, ov, in_sems, out_sems):
    parts, rows, blk = tv.shape
    cols = pl.ds(pl.multiple_of(lax.axis_index("section") * blk, HEAD), blk)
    spans = row_chunks(rows, chunks)
    loads, stores = [], []
    for c, span in enumerate(spans):
        loads.append(
            (
                pltpu.make_async_copy(t_hbm.at[:, span], tv.at[:, span], in_sems.at[2 * c]),
                pltpu.make_async_copy(up_hbm.at[span, cols], uv.at[span], in_sems.at[2 * c + 1]),
            )
        )
        for one in loads[c]:
            one.start()
    for c, span in enumerate(spans):
        for one in loads[c]:
            one.wait()
        total = uv[span, :].astype(jnp.float32)
        for s in reversed(range(parts)):
            total = total + tv[s, span, :].astype(jnp.float32)
            ov[s, span, :] = total.astype(jnp.bfloat16)
        stores.append(pltpu.make_async_copy(ov.at[:, span], out_hbm.at[:, span], out_sems.at[c]))
        stores[c].start()
    for one in stores:
        one.wait()


def row_chunks(rows, count):
    step = rows // count
    return [pl.ds(c * step, step) for c in range(count)]


def suffix_sums(got, upstream, after):
    parts, rows, blk = got.shape
    chunks = 4
    anywhere = pl.BlockSpec(memory_space=pl.ANY)
    return pl.pallas_call(
        lambda *refs: suffix_kernel(chunks, *refs),
        in_specs=[anywhere] * 3,
        out_specs=anywhere,
        out_shape=jax.ShapeDtypeStruct(got.shape, jnp.bfloat16),
        scratch_shapes=[
            pltpu.VMEM(got.shape, jnp.bfloat16),
            pltpu.VMEM((rows, blk), jnp.bfloat16),
            pltpu.VMEM(got.shape, jnp.bfloat16),
            pltpu.SemaphoreType.DMA((2 * chunks,)),
            pltpu.SemaphoreType.DMA((chunks,)),
        ],
        compiler_params=params(60),
        cost_estimate=cost(parts * rows * blk, 4 * parts * rows * blk),
        name="suffix_sums",
    )(got, upstream, after)


def lay_kernel(in_ref, out_ref):
    blk = in_ref.shape[2]
    for p in range(in_ref.shape[0]):
        out_ref[:, p * blk : (p + 1) * blk] = in_ref[p]


def side_by_side(got):
    parts, rows, blk = got.shape
    some = parts // 2
    return pl.pallas_call(
        lay_kernel,
        grid=(2,),
        in_specs=[pl.BlockSpec((some, rows, blk), lambda i: (i, 0, 0))],
        out_specs=pl.BlockSpec((rows, some * blk), lambda i: (0, i)),
        out_shape=jax.ShapeDtypeStruct((rows, parts * blk), got.dtype),
        compiler_params=params(16),
        cost_estimate=cost(0, 4 * parts * rows * blk),
        name="side_by_side",
    )(got)


def wgrad_kernel(x_hbm, up, down, far, k0, k1, k3, k2, keep_hbm, send_hbm, av, kv, full, low, in_sems, out_sems):
    rows, wide = up.shape
    blk = wide // 2
    half = blk // 2
    loads = []
    for n, k in enumerate((k0, k1, k3, k2)):
        loads.append(pltpu.make_async_copy(k, kv.at[pl.ds(n * rows, rows)], in_sems.at[n]))
        loads[n].start()
    cols = chip_columns(blk, 0)
    parts = []
    for y in range(2):
        span = pl.ds(y * blk, blk)
        srcs = (x_hbm.at[:, cols[y]], up.at[:, span], down.at[:, span], far.at[:, span])
        group = []
        for n, src in enumerate(srcs):
            dst = av.at[pl.ds(n * rows, rows), span]
            group.append(pltpu.make_async_copy(src, dst, in_sems.at[4 + 4 * y + n]))
            group[n].start()
        parts.append(group)
    for one in loads:
        one.wait()
    core = lax.rem(lax.axis_index("dp"), 2)
    own = pl.multiple_of(core * half, half)
    other = pl.multiple_of((1 - core) * half, half)
    stores = []
    for y in range(2):
        for one in parts[y]:
            one.wait()
        full[y] = lax.dot_general(
            av[:, y * blk : (y + 1) * blk], kv[...], (((0,), (0,)), ((), ())), preferred_element_type=jnp.float32
        )
        low[y] = full[y, pl.ds(other, half), :].astype(jnp.bfloat16)
        stores.append(pltpu.make_async_copy(full.at[y, pl.ds(own, half)], keep_hbm.at[y], out_sems.at[2 * y]))
        stores.append(pltpu.make_async_copy(low.at[y], send_hbm.at[y], out_sems.at[2 * y + 1]))
        stores[2 * y].start()
        stores[2 * y + 1].start()
    for one in stores:
        one.wait()


def wgrad(acts, got, kgs, got_kgs):
    rows, width = acts.shape
    blk = width // (2 * NX)
    kv = kgs.shape[1]
    half = blk // 2
    anywhere = pl.BlockSpec(memory_space=pl.ANY)
    return pl.pallas_call(
        wgrad_kernel,
        in_specs=[anywhere] * 8,
        out_specs=[anywhere, anywhere],
        scratch_shapes=[
            pltpu.VMEM((4 * rows, 2 * blk), jnp.bfloat16),
            pltpu.VMEM((4 * rows, kv), jnp.bfloat16),
            pltpu.VMEM((2, blk, kv), jnp.float32),
            pltpu.VMEM((2, half, kv), jnp.bfloat16),
            pltpu.SemaphoreType.DMA((12,)),
            pltpu.SemaphoreType.DMA((4,)),
        ],
        out_shape=[
            jax.ShapeDtypeStruct((2, half, kv), jnp.float32),
            jax.ShapeDtypeStruct((2, half, kv), jnp.bfloat16),
        ],
        compiler_params=params(40),
        cost_estimate=cost(2 * 4 * rows * 2 * blk * kv, 2 * 4 * rows * (2 * blk + kv)),
        name="wgrad",
    )(acts, *got, kgs, *got_kgs)


def merge_kernel(keep, got, here_ref, there_ref):
    y = lax.axis_index("dp") // 8
    here_ref[...] = keep[y] + got[y].astype(jnp.float32)
    there_ref[...] = (keep[1 - y] + got[1 - y].astype(jnp.float32)).astype(jnp.bfloat16)


def merge(keep, got):
    two, half, kv = keep.shape
    inside = pl.BlockSpec(memory_space=pltpu.VMEM)
    return pl.pallas_call(
        merge_kernel,
        in_specs=[inside, inside],
        out_shape=[
            jax.ShapeDtypeStruct((half, kv), jnp.float32),
            jax.ShapeDtypeStruct((half, kv), jnp.bfloat16),
        ],
        compiler_params=params(16),
        cost_estimate=cost(2 * half * kv, 18 * half * kv),
        name="merge",
    )(keep, got)


def adam_kernel(here, got, gain, master, first, second, o_master, o_first, o_second, o_weight):
    grad = gain[...] * (here[...] + got[...].astype(jnp.float32))
    new_first = beta_one * first[0] + (1.0 - beta_one) * grad
    new_second = beta_two * second[0] + (1.0 - beta_two) * grad * grad
    corr_one = 1.0 - beta_one**10
    corr_two = 1.0 - beta_two**10
    update = (
        new_first / corr_one / (jnp.sqrt(new_second / corr_two) + adam_eps)
        + decay_rate * master[0]
    )
    new_master = master[0] - learn_rate * update
    o_master[0] = new_master
    o_first[0] = new_first
    o_second[0] = new_second
    o_weight[...] = new_master.astype(jnp.bfloat16)


def adam(here, got, gain, master, first, second):
    half, kv = here.shape
    tile = half // 2
    flat = pl.BlockSpec((tile, kv), lambda i: (i, 0))
    deep = pl.BlockSpec((1, tile, kv), lambda i: (0, i, 0))
    out = jax.ShapeDtypeStruct(master.shape, jnp.float32)
    return pl.pallas_call(
        adam_kernel,
        grid=(2,),
        in_specs=[flat, flat, pl.BlockSpec((tile, 1), lambda i: (i, 0)), deep, deep, deep],
        out_specs=[deep, deep, deep, flat],
        out_shape=[out, out, out, jax.ShapeDtypeStruct((half, kv), jnp.bfloat16)],
        compiler_params=params(16),
        cost_estimate=cost(20 * half * kv, 32 * half * kv),
        name="adam",
    )(here, got, gain, master, first, second)


def place(plan, bases, blocks, rows, kv, whole):
    prior = [] if whole is None else [whole]
    count = len(blocks)
    block = rows // 16

    def kernel(base_ref, *refs):
        ins, out, sems = refs[:count], refs[-2], refs[-1]
        moves = []
        for which, index, slot in plan:
            at = pl.multiple_of(base_ref[slot], 32)
            moves.append((ins[which].at[pl.ds(index, block)], out.at[pl.ds(at, block)]))
        run_copies(moves, sems)

    return pl.pallas_call(
        kernel,
        in_specs=[pl.BlockSpec(memory_space=pltpu.SMEM)]
        + [pl.BlockSpec(memory_space=pltpu.VMEM)] * count
        + [pl.BlockSpec(memory_space=pl.ANY)] * len(prior),
        out_specs=pl.BlockSpec(memory_space=pl.ANY),
        out_shape=jax.ShapeDtypeStruct((rows, kv), jnp.bfloat16),
        scratch_shapes=[pltpu.SemaphoreType.DMA((len(plan),))],
        input_output_aliases={} if whole is None else {1 + count: 0},
        compiler_params=params(16),
        cost_estimate=cost(0, 4 * kv * len(plan) * block),
        name="place",
    )(bases, *blocks, *prior)


def spread(slots, bases, blocks, rows):
    count = len(blocks)
    block, kv = blocks[0].shape

    def kernel(base_ref, *refs):
        ins, (stack, whole, sems) = refs[:count], refs[count:]
        moves = []
        for n, slot in enumerate(slots):
            at = pl.multiple_of(base_ref[slot], 32)
            moves.append((ins[n], stack.at[pl.ds(n * block, block)]))
            moves.append((ins[n], whole.at[pl.ds(at, block)]))
        run_copies(moves, sems)

    return pl.pallas_call(
        kernel,
        in_specs=[pl.BlockSpec(memory_space=pltpu.SMEM)]
        + [pl.BlockSpec(memory_space=pltpu.VMEM)] * count,
        out_specs=[pl.BlockSpec(memory_space=pl.ANY)] * 2,
        out_shape=[
            jax.ShapeDtypeStruct((count * block, kv), jnp.bfloat16),
            jax.ShapeDtypeStruct((rows, kv), jnp.bfloat16),
        ],
        scratch_shapes=[pltpu.SemaphoreType.DMA((2 * count,))],
        compiler_params=params(16),
        cost_estimate=cost(0, 6 * count * block * kv),
        name="spread",
    )(bases, *blocks)


def gather_rows(own, y, x, core):
    rows, kv = own.shape
    send = lambda block, perm: lax.ppermute(block, "dp", perm)
    up, down = along_x(1), along_x(-1)
    yr = send(own, SWAP_Y)
    a = send(own, up)
    b = send(own, down)
    e = send(own, along_x(2))
    later, a, b = lax.optimization_barrier((yr, a, b))
    a2 = send(later, up)
    b2 = send(later, down)
    latest, e = lax.optimization_barrier((yr, e))
    e2 = send(latest, along_x(2))
    order = (0, -1, 1, 2)
    table = []
    for dy in range(2):
        for dx in order:
            for dc in range(2):
                yy = y if dy == 0 else 1 - y
                cc = core if dc == 0 else 1 - core
                table.append((yy * 8 + lax.rem(x + dx + NX, NX) * 2 + cc) * rows)
    bases = jnp.stack(table).astype(jnp.int32)

    def put(entries, whole, others=()):
        blocks = [one[0] for one in entries]
        plan = []
        for n, (block, dy, dx) in enumerate(entries):
            plan.append((n, 0, (dy * 4 + order.index(dx)) * 2))
        for group, swapped in others:
            for n, (block, dy, dx) in enumerate(group):
                slot = (dy * 4 + order.index(dx)) * 2 + 1
                one = 0 if len(swapped) == 1 else n
                plan.append((len(blocks) + one, (n - one) * rows, slot))
            blocks = blocks + swapped
        return place(plan, bases, blocks, 16 * rows, kv, whole)

    near = [(own, 0, 0), (a, 0, -1), (b, 0, 1)]
    slots = [(dy * 4 + order.index(dx)) * 2 for _, dy, dx in near]
    stack, whole = spread(slots, bases, [one[0] for one in near], 16 * rows)
    early = [send(yr, SWAP_CORE), send(e, SWAP_CORE)]
    a2, stack, early[0] = lax.optimization_barrier((a2, stack, early[0]))
    e2, early[1] = lax.optimization_barrier((e2, early[1]))
    middle = [(a2, 1, -1), (b2, 1, 1), (e2, 1, 2)]
    swapped = [send(one[0], SWAP_CORE) for one in middle]
    stack, swapped[0], swapped[1], swapped[2] = lax.optimization_barrier((stack, swapped[0], swapped[1], swapped[2]))
    c1 = send(stack, SWAP_CORE)
    middle += [(yr, 1, 0), (e, 0, 2)]
    whole = put(middle, whole, [(middle, swapped + early)])
    return put([], whole, [(near, [c1])])


def body(
    activations,
    norm_gain,
    key_weight,
    key_gain,
    key_cotangent,
    upstream,
    master,
    first_moment,
    second_moment,
):
    sections = lax.axis_size("section")
    micro, tok, width = activations.shape[1:]
    rows = micro * tok
    acts = activations.reshape(rows, width)
    weight = key_weight[0]
    kv = weight.shape[1]
    me = lax.axis_index("dp")
    y, x, core = me // 8, lax.rem(me // 2, NX), lax.rem(me, 2)
    upstream = upstream.reshape(rows, width)

    cut = cut_columns(acts)
    got = [lax.ppermute(one, "dp", along_x(k)) for one, k in zip(cut, (1, -1, 2))]
    kgs, term = front(acts, norm_gain, weight, key_gain, key_cotangent.reshape(rows, kv), sections, cut[0])
    got_kgs = [lax.ppermute(kgs, "dp", along_x(1)), lax.ppermute(kgs, "dp", along_x(-1))]
    kgs_late, *got = lax.optimization_barrier((kgs, *got))
    got_kgs.append(lax.ppermute(kgs_late, "dp", along_x(2)))
    theirs = lax.all_to_all(term, "section", 0, 0)

    keep, away = wgrad(acts, got, kgs, got_kgs)
    here, there = merge(keep, lax.ppermute(away, "dp", SWAP_CORE))
    sums = suffix_sums(theirs, upstream, here)
    mine = lax.all_to_all(sums, "section", 0, 0)
    input_grad = side_by_side(mine).reshape(activations.shape)

    own_rows = here.shape[0]
    gain_rows = lax.dynamic_slice(norm_gain[0], (me * own_rows,), (own_rows,))[:, None]
    new_master, new_first, new_second, own = adam(
        here, lax.ppermute(there, "dp", SWAP_Y), gain_rows, master, first_moment, second_moment
    )
    new_weight = gather_rows(own, y, x, core)
    return (input_grad, new_weight[None], new_master, new_first, new_second)


def solution(mesh):
    return jax.shard_map(
        body,
        mesh=mesh,
        in_specs=(
            P("section", None, "dp", None),
            P("section", None),
            P("section", None, None),
            P("section", None),
            P("section", None, "dp", None),
            P(None, "dp", None),
            P("section", "dp", None),
            P("section", "dp", None),
            P("section", "dp", None),
        ),
        out_specs=(
            P("section", None, "dp", None),
            P("section", None, None),
            P("section", "dp", None),
            P("section", "dp", None),
            P("section", "dp", None),
        ),
        check_vma=False,
    )
```

```python
import jax
import jax.numpy as jnp
from jax import lax
from jax.experimental import pallas as pl
from jax.experimental.pallas import tpu as pltpu
from jax.sharding import PartitionSpec as P

HEAD = 128
HEADS_KV = 4

beta_one = 0.9
beta_two = 0.95
learn_rate = 0.002
decay_rate = 0.1
adam_eps = 1e-08

NX = 4
FRONT_CHUNKS = 4


def along_x(k):
    return [(i, (i & 8) | ((((i >> 1) & 3) + k) % NX) * 2 | (i & 1)) for i in range(16)]


SWAP_CORE = [(i, i ^ 1) for i in range(16)]
SWAP_Y = [(i, i ^ 8) for i in range(16)]


def params(mib):
    return pltpu.CompilerParams(vmem_limit_bytes=mib * 1024 * 1024)


def cost(flops, nbytes):
    return pl.CostEstimate(flops=0, bytes_accessed=1, transcendentals=0)


def chip_columns(blk, k):
    x = lax.rem(lax.axis_index("dp") // 2 + k, NX)
    return [pl.ds(pl.multiple_of((y * NX + x) * blk, HEAD), blk) for y in range(2)]


def run_copies(moves, sems):
    copies = [pltpu.make_async_copy(src, dst, sems.at[n]) for n, (src, dst) in enumerate(moves)]
    for one in copies:
        one.start()
    for one in copies:
        one.wait()


def cut_kernel(x_hbm, up, down, far, sems):
    blk = up.shape[1] // 2
    moves = []
    for out, k in ((up, 1), (down, NX - 1), (far, 2)):
        for y, cols in enumerate(chip_columns(blk, k)):
            moves.append((x_hbm.at[:, cols], out.at[:, pl.ds(y * blk, blk)]))
    run_copies(moves, sems)


def cut_columns(acts):
    rows, width = acts.shape
    out = jax.ShapeDtypeStruct((rows, width // NX), acts.dtype)
    return pl.pallas_call(
        cut_kernel,
        in_specs=[pl.BlockSpec(memory_space=pl.ANY)],
        out_specs=[pl.BlockSpec(memory_space=pltpu.VMEM)] * 3,
        out_shape=[out] * 3,
        scratch_shapes=[pltpu.SemaphoreType.DMA((6,))],
        compiler_params=params(60),
        cost_estimate=cost(0, 12 * rows * width // NX),
        name="cut_columns",
    )(acts)


def front_kernel(parts, x_hbm, w_hbm, gain_ref, hgain_ref, cot_ref, after_ref, kgs_ref, term_hbm, xv, wv, tv, acc, kgv, in_sems, out_sems):
    rows, width = xv.shape
    step = width // FRONT_CHUNKS
    spans = [pl.ds(c * step, step) for c in range(FRONT_CHUNKS)]
    loads = []
    for c, span in enumerate(spans):
        loads.append(
            (
                pltpu.make_async_copy(x_hbm.at[:, span], xv.at[:, span], in_sems.at[2 * c]),
                pltpu.make_async_copy(w_hbm.at[span], wv.at[span], in_sems.at[2 * c + 1]),
            )
        )
    for pair in loads:
        for one in pair:
            one.start()
    ssq = None
    for c, span in enumerate(spans):
        for one in loads[c]:
            one.wait()
        xf = xv[:, span].astype(jnp.float32)
        scaled = (xf * gain_ref[:, span]).astype(jnp.bfloat16)
        part = jnp.dot(scaled, wv[span, :], preferred_element_type=jnp.float32)
        sq = jnp.sum(xf * xf, axis=-1, keepdims=True)
        if c == 0:
            acc[...] = part
            ssq = sq
        else:
            acc[...] += part
            ssq = ssq + sq
    inv = lax.rsqrt(ssq / width + 1e-06)
    hg = hgain_ref[...]
    dots = jnp.zeros_like(inv)
    for h in range(HEADS_KV):
        cols = slice(h * HEAD, (h + 1) * HEAD)
        raw = acc[:, cols] * inv
        hinv = lax.rsqrt(jnp.mean(raw * raw, axis=-1, keepdims=True) + 1e-06)
        scaled = cot_ref[:, cols].astype(jnp.float32) * hg
        kg = hinv * (scaled - raw * hinv * hinv * jnp.mean(scaled * raw, axis=-1, keepdims=True))
        kgs_ref[:, cols] = (kg * inv).astype(jnp.bfloat16)
        kg = kg.astype(jnp.bfloat16)
        kgv[:, cols] = kg
        dots += jnp.sum(kg.astype(jnp.float32) * raw, axis=-1, keepdims=True)
    coef = inv * inv * dots / width
    stores = []
    blk = width // parts
    for c in range(parts):
        span = pl.ds(c * blk, blk)
        back = lax.dot_general(
            kgv[...], wv[span, :], (((1,), (1,)), ((), ())), preferred_element_type=jnp.float32
        )
        term = inv * (gain_ref[:, span] * back) - coef * xv[:, span].astype(jnp.float32)
        tv[c] = term.astype(jnp.bfloat16)
        stores.append(pltpu.make_async_copy(tv.at[c], term_hbm.at[c], out_sems.at[c]))
        stores[c].start()
    for one in stores:
        one.wait()


def front(acts, gain, weight, head_gain, cot, parts, after):
    rows, width = acts.shape
    kv = weight.shape[1]
    blk = width // parts
    anywhere = pl.BlockSpec(memory_space=pl.ANY)
    inside = pl.BlockSpec(memory_space=pltpu.VMEM)
    return pl.pallas_call(
        lambda *refs: front_kernel(parts, *refs),
        in_specs=[anywhere, anywhere, inside, inside, inside, anywhere],
        out_specs=[inside, anywhere],
        out_shape=[
            jax.ShapeDtypeStruct((rows, kv), jnp.bfloat16),
            jax.ShapeDtypeStruct((parts, rows, blk), jnp.bfloat16),
        ],
        scratch_shapes=[
            pltpu.VMEM((rows, width), jnp.bfloat16),
            pltpu.VMEM((width, kv), jnp.bfloat16),
            pltpu.VMEM((parts, rows, blk), jnp.bfloat16),
            pltpu.VMEM((rows, kv), jnp.float32),
            pltpu.VMEM((rows, kv), jnp.bfloat16),
            pltpu.SemaphoreType.DMA((2 * FRONT_CHUNKS,)),
            pltpu.SemaphoreType.DMA((parts,)),
        ],
        compiler_params=params(60),
        cost_estimate=cost(40 * rows * width * kv, 2 * width * (2 * rows + kv)),
        name="front",
    )(acts, weight, gain, head_gain, cot, after)


def row_chunks(rows, count):
    step = rows // count
    return [pl.ds(c * step, step) for c in range(count)]


def suffix_kernel(chunks, t_hbm, up_hbm, after_ref, out_hbm, tv, uv, ov, in_sems, out_sems):
    parts, rows, blk = tv.shape
    cols = pl.ds(pl.multiple_of(lax.axis_index("section") * blk, HEAD), blk)
    spans = row_chunks(rows, chunks)
    loads, stores = [], []
    for c, span in enumerate(spans):
        loads.append(
            (
                pltpu.make_async_copy(t_hbm.at[:, span], tv.at[:, span], in_sems.at[2 * c]),
                pltpu.make_async_copy(up_hbm.at[span, cols], uv.at[span], in_sems.at[2 * c + 1]),
            )
        )
        for one in loads[c]:
            one.start()
    for c, span in enumerate(spans):
        for one in loads[c]:
            one.wait()
        total = uv[span, :].astype(jnp.float32)
        for s in reversed(range(parts)):
            total = total + tv[s, span, :].astype(jnp.float32)
            ov[s, span, :] = total.astype(jnp.bfloat16)
        stores.append(pltpu.make_async_copy(ov.at[:, span], out_hbm.at[:, span], out_sems.at[c]))
        stores[c].start()
    for one in stores:
        one.wait()


def row_chunks(rows, count):
    step = rows // count
    return [pl.ds(c * step, step) for c in range(count)]


def suffix_sums(got, upstream, after):
    parts, rows, blk = got.shape
    chunks = 4
    anywhere = pl.BlockSpec(memory_space=pl.ANY)
    return pl.pallas_call(
        lambda *refs: suffix_kernel(chunks, *refs),
        in_specs=[anywhere] * 3,
        out_specs=anywhere,
        out_shape=jax.ShapeDtypeStruct(got.shape, jnp.bfloat16),
        scratch_shapes=[
            pltpu.VMEM(got.shape, jnp.bfloat16),
            pltpu.VMEM((rows, blk), jnp.bfloat16),
            pltpu.VMEM(got.shape, jnp.bfloat16),
            pltpu.SemaphoreType.DMA((2 * chunks,)),
            pltpu.SemaphoreType.DMA((chunks,)),
        ],
        compiler_params=params(60),
        cost_estimate=cost(parts * rows * blk, 4 * parts * rows * blk),
        name="suffix_sums",
    )(got, upstream, after)


def wgrad_kernel(x_hbm, up, down, far, k0, k1, k3, k2, keep_hbm, send_hbm, av, kv, full, low, in_sems, out_sems):
    rows, wide = up.shape
    blk = wide // 2
    half = blk // 2
    loads = []
    for n, k in enumerate((k0, k1, k3, k2)):
        loads.append(pltpu.make_async_copy(k, kv.at[pl.ds(n * rows, rows)], in_sems.at[n]))
        loads[n].start()
    cols = chip_columns(blk, 0)
    parts = []
    for y in range(2):
        span = pl.ds(y * blk, blk)
        srcs = (x_hbm.at[:, cols[y]], up.at[:, span], down.at[:, span], far.at[:, span])
        group = []
        for n, src in enumerate(srcs):
            dst = av.at[pl.ds(n * rows, rows), span]
            group.append(pltpu.make_async_copy(src, dst, in_sems.at[4 + 4 * y + n]))
            group[n].start()
        parts.append(group)
    for one in loads:
        one.wait()
    core = lax.rem(lax.axis_index("dp"), 2)
    own = pl.multiple_of(core * half, half)
    other = pl.multiple_of((1 - core) * half, half)
    stores = []
    for y in range(2):
        for one in parts[y]:
            one.wait()
        full[y] = lax.dot_general(
            av[:, y * blk : (y + 1) * blk], kv[...], (((0,), (0,)), ((), ())), preferred_element_type=jnp.float32
        )
        low[y] = full[y, pl.ds(other, half), :].astype(jnp.bfloat16)
        stores.append(pltpu.make_async_copy(full.at[y, pl.ds(own, half)], keep_hbm.at[y], out_sems.at[2 * y]))
        stores.append(pltpu.make_async_copy(low.at[y], send_hbm.at[y], out_sems.at[2 * y + 1]))
        stores[2 * y].start()
        stores[2 * y + 1].start()
    for one in stores:
        one.wait()


def wgrad(acts, got, kgs, got_kgs):
    rows, width = acts.shape
    blk = width // (2 * NX)
    kv = kgs.shape[1]
    half = blk // 2
    anywhere = pl.BlockSpec(memory_space=pl.ANY)
    return pl.pallas_call(
        wgrad_kernel,
        in_specs=[anywhere] * 8,
        out_specs=[anywhere, anywhere],
        scratch_shapes=[
            pltpu.VMEM((4 * rows, 2 * blk), jnp.bfloat16),
            pltpu.VMEM((4 * rows, kv), jnp.bfloat16),
            pltpu.VMEM((2, blk, kv), jnp.float32),
            pltpu.VMEM((2, half, kv), jnp.bfloat16),
            pltpu.SemaphoreType.DMA((12,)),
            pltpu.SemaphoreType.DMA((4,)),
        ],
        out_shape=[
            jax.ShapeDtypeStruct((2, half, kv), jnp.float32),
            jax.ShapeDtypeStruct((2, half, kv), jnp.bfloat16),
        ],
        compiler_params=params(40),
        cost_estimate=cost(2 * 4 * rows * 2 * blk * kv, 2 * 4 * rows * (2 * blk + kv)),
        name="wgrad",
    )(acts, *got, kgs, *got_kgs)


def merge_kernel(keep, got, here_ref, there_ref):
    y = lax.axis_index("dp") // 8
    here_ref[...] = keep[y] + got[y].astype(jnp.float32)
    there_ref[...] = (keep[1 - y] + got[1 - y].astype(jnp.float32)).astype(jnp.bfloat16)


def merge(keep, got):
    two, half, kv = keep.shape
    inside = pl.BlockSpec(memory_space=pltpu.VMEM)
    return pl.pallas_call(
        merge_kernel,
        in_specs=[inside, inside],
        out_shape=[
            jax.ShapeDtypeStruct((half, kv), jnp.float32),
            jax.ShapeDtypeStruct((half, kv), jnp.bfloat16),
        ],
        compiler_params=params(16),
        cost_estimate=cost(2 * half * kv, 18 * half * kv),
        name="merge",
    )(keep, got)


def adam_kernel(here, got, gain, master, first, second, o_master, o_first, o_second, o_weight):
    grad = gain[...] * (here[...] + got[...].astype(jnp.float32))
    new_first = beta_one * first[0] + (1.0 - beta_one) * grad
    new_second = beta_two * second[0] + (1.0 - beta_two) * grad * grad
    corr_one = 1.0 - beta_one**10
    corr_two = 1.0 - beta_two**10
    update = (
        new_first / corr_one / (jnp.sqrt(new_second / corr_two) + adam_eps)
        + decay_rate * master[0]
    )
    new_master = master[0] - learn_rate * update
    o_master[0] = new_master
    o_first[0] = new_first
    o_second[0] = new_second
    o_weight[...] = new_master.astype(jnp.bfloat16)


def adam(here, got, gain, master, first, second):
    half, kv = here.shape
    tile = half // 2
    flat = pl.BlockSpec((tile, kv), lambda i: (i, 0))
    deep = pl.BlockSpec((1, tile, kv), lambda i: (0, i, 0))
    out = jax.ShapeDtypeStruct(master.shape, jnp.float32)
    return pl.pallas_call(
        adam_kernel,
        grid=(2,),
        in_specs=[flat, flat, pl.BlockSpec((tile, 1), lambda i: (i, 0)), deep, deep, deep],
        out_specs=[deep, deep, deep, flat],
        out_shape=[out, out, out, jax.ShapeDtypeStruct((half, kv), jnp.bfloat16)],
        compiler_params=params(16),
        cost_estimate=cost(20 * half * kv, 32 * half * kv),
        name="adam",
    )(here, got, gain, master, first, second)


def place(plan, bases, blocks, rows, kv, whole):
    prior = [] if whole is None else [whole]
    count = len(blocks)
    block = rows // 16

    def kernel(base_ref, *refs):
        ins, out, sems = refs[:count], refs[-2], refs[-1]
        moves = []
        for which, index, slot in plan:
            at = pl.multiple_of(base_ref[slot], 32)
            moves.append((ins[which].at[pl.ds(index, block)], out.at[pl.ds(at, block)]))
        run_copies(moves, sems)

    return pl.pallas_call(
        kernel,
        in_specs=[pl.BlockSpec(memory_space=pltpu.SMEM)]
        + [pl.BlockSpec(memory_space=pltpu.VMEM)] * count
        + [pl.BlockSpec(memory_space=pl.ANY)] * len(prior),
        out_specs=pl.BlockSpec(memory_space=pl.ANY),
        out_shape=jax.ShapeDtypeStruct((rows, kv), jnp.bfloat16),
        scratch_shapes=[pltpu.SemaphoreType.DMA((len(plan),))],
        input_output_aliases={} if whole is None else {1 + count: 0},
        compiler_params=params(60),
        cost_estimate=cost(0, 4 * kv * len(plan) * block),
        name="place",
    )(bases, *blocks, *prior)


def finish(slots, bases, late, got, whole):
    parts, rows, blk = got.shape
    some = parts // 2
    count = len(slots)
    block = late.shape[0] // count

    def kernel(base_ref, late_ref, got_ref, whole_ref, out, wide_ref, sems):
        copies = []
        for n, slot in enumerate(slots):
            at = pl.multiple_of(base_ref[slot], 32)
            src = late_ref.at[pl.ds(n * block, block)]
            copies.append(pltpu.make_async_copy(src, out.at[pl.ds(at, block)], sems.at[n]))

        @pl.when(pl.program_id(0) == 0)
        def _():
            for one in copies:
                one.start()

        for p in range(some):
            wide_ref[:, p * blk : (p + 1) * blk] = got_ref[p]

        @pl.when(pl.program_id(0) == 1)
        def _():
            for one in copies:
                one.wait()

    return pl.pallas_call(
        kernel,
        grid=(2,),
        in_specs=[
            pl.BlockSpec(memory_space=pltpu.SMEM),
            pl.BlockSpec(late.shape, lambda i: (0, 0)),
            pl.BlockSpec((some, rows, blk), lambda i: (i, 0, 0)),
            pl.BlockSpec(memory_space=pl.ANY),
        ],
        out_specs=[
            pl.BlockSpec(memory_space=pl.ANY),
            pl.BlockSpec((rows, some * blk), lambda i: (0, i)),
        ],
        out_shape=[
            jax.ShapeDtypeStruct(whole.shape, whole.dtype),
            jax.ShapeDtypeStruct((rows, parts * blk), got.dtype),
        ],
        scratch_shapes=[pltpu.SemaphoreType.DMA((count,))],
        input_output_aliases={3: 0},
        compiler_params=params(16),
        cost_estimate=cost(0, 4 * got.size),
        name="finish",
    )(bases, late, got, whole)


def spread(slots, bases, blocks, rows):
    count = len(blocks)
    block, kv = blocks[0].shape

    def kernel(base_ref, *refs):
        ins, (stack, whole, sems) = refs[:count], refs[count:]
        moves = []
        for n, slot in enumerate(slots):
            at = pl.multiple_of(base_ref[slot], 32)
            moves.append((ins[n], stack.at[pl.ds(n * block, block)]))
            moves.append((ins[n], whole.at[pl.ds(at, block)]))
        run_copies(moves, sems)

    return pl.pallas_call(
        kernel,
        in_specs=[pl.BlockSpec(memory_space=pltpu.SMEM)]
        + [pl.BlockSpec(memory_space=pltpu.VMEM)] * count,
        out_specs=[pl.BlockSpec(memory_space=pl.ANY)] * 2,
        out_shape=[
            jax.ShapeDtypeStruct((count * block, kv), jnp.bfloat16),
            jax.ShapeDtypeStruct((rows, kv), jnp.bfloat16),
        ],
        scratch_shapes=[pltpu.SemaphoreType.DMA((2 * count,))],
        compiler_params=params(16),
        cost_estimate=cost(0, 6 * count * block * kv),
        name="spread",
    )(bases, *blocks)


def gather_rows(own, y, x, core, mine):
    rows, kv = own.shape
    send = lambda block, perm: lax.ppermute(block, "dp", perm)
    up, down = along_x(1), along_x(-1)
    yr = send(own, SWAP_Y)
    a = send(own, up)
    b = send(own, down)
    e = send(own, along_x(2))
    later, a, b = lax.optimization_barrier((yr, a, b))
    a2 = send(later, up)
    b2 = send(later, down)
    latest, e = lax.optimization_barrier((yr, e))
    e2 = send(latest, along_x(2))
    order = (0, -1, 1, 2)
    table = []
    for dy in range(2):
        for dx in order:
            for dc in range(2):
                yy = y if dy == 0 else 1 - y
                cc = core if dc == 0 else 1 - core
                table.append((yy * 8 + lax.rem(x + dx + NX, NX) * 2 + cc) * rows)
    bases = jnp.stack(table).astype(jnp.int32)

    def put(entries, whole, others=()):
        blocks = [one[0] for one in entries]
        plan = []
        for n, (block, dy, dx) in enumerate(entries):
            plan.append((n, 0, (dy * 4 + order.index(dx)) * 2))
        for group, swapped in others:
            for n, (block, dy, dx) in enumerate(group):
                slot = (dy * 4 + order.index(dx)) * 2 + 1
                one = 0 if len(swapped) == 1 else n
                plan.append((len(blocks) + one, (n - one) * rows, slot))
            blocks = blocks + swapped
        return place(plan, bases, blocks, 16 * rows, kv, whole)

    near = [(own, 0, 0), (a, 0, -1), (b, 0, 1)]
    slots = [(dy * 4 + order.index(dx)) * 2 for _, dy, dx in near]
    stack, whole = spread(slots, bases, [one[0] for one in near], 16 * rows)
    early = [send(yr, SWAP_CORE), send(e, SWAP_CORE)]
    a2, stack, early[0] = lax.optimization_barrier((a2, stack, early[0]))
    e2, early[1] = lax.optimization_barrier((e2, early[1]))
    middle = [(a2, 1, -1), (b2, 1, 1), (e2, 1, 2)]
    swapped = [send(one[0], SWAP_CORE) for one in middle]
    stack, swapped[0], swapped[1], swapped[2] = lax.optimization_barrier((stack, swapped[0], swapped[1], swapped[2]))
    c1 = send(stack, SWAP_CORE)
    middle += [(yr, 1, 0), (e, 0, 2)]
    whole = put(middle, whole, [(middle, swapped + early)])
    slots = [slot + 1 for slot in slots]
    return finish(slots, bases, c1, mine, whole)


def body(
    activations,
    norm_gain,
    key_weight,
    key_gain,
    key_cotangent,
    upstream,
    master,
    first_moment,
    second_moment,
):
    sections = lax.axis_size("section")
    micro, tok, width = activations.shape[1:]
    rows = micro * tok
    acts = activations.reshape(rows, width)
    weight = key_weight[0]
    kv = weight.shape[1]
    me = lax.axis_index("dp")
    y, x, core = me // 8, lax.rem(me // 2, NX), lax.rem(me, 2)
    upstream = upstream.reshape(rows, width)

    cut = cut_columns(acts)
    got = [lax.ppermute(one, "dp", along_x(k)) for one, k in zip(cut, (1, -1, 2))]
    kgs, term = front(acts, norm_gain, weight, key_gain, key_cotangent.reshape(rows, kv), sections, cut[0])
    got_kgs = [lax.ppermute(kgs, "dp", along_x(1)), lax.ppermute(kgs, "dp", along_x(-1))]
    kgs_late, *got = lax.optimization_barrier((kgs, *got))
    got_kgs.append(lax.ppermute(kgs_late, "dp", along_x(2)))
    theirs = lax.all_to_all(term, "section", 0, 0)

    keep, away = wgrad(acts, got, kgs, got_kgs)
    here, there = merge(keep, lax.ppermute(away, "dp", SWAP_CORE))
    sums = suffix_sums(theirs, upstream, here)
    mine = lax.all_to_all(sums, "section", 0, 0)

    own_rows = here.shape[0]
    gain_rows = lax.dynamic_slice(norm_gain[0], (me * own_rows,), (own_rows,))[:, None]
    new_master, new_first, new_second, own = adam(
        here, lax.ppermute(there, "dp", SWAP_Y), gain_rows, master, first_moment, second_moment
    )
    new_weight, input_grad = gather_rows(own, y, x, core, mine)
    return (input_grad.reshape(activations.shape), new_weight[None], new_master, new_first, new_second)


def solution(mesh):
    return jax.shard_map(
        body,
        mesh=mesh,
        in_specs=(
            P("section", None, "dp", None),
            P("section", None),
            P("section", None, None),
            P("section", None),
            P("section", None, "dp", None),
            P(None, "dp", None),
            P("section", "dp", None),
            P("section", "dp", None),
            P("section", "dp", None),
        ),
        out_specs=(
            P("section", None, "dp", None),
            P("section", None, None),
            P("section", "dp", None),
            P("section", "dp", None),
            P("section", "dp", None),
        ),
        check_vma=False,
    )
```

```python
import jax
import jax.numpy as jnp
from jax import lax
from jax.experimental import pallas as pl
from jax.experimental.pallas import tpu as pltpu
from jax.sharding import PartitionSpec as P

HEAD = 128
HEADS_KV = 4

beta_one = 0.9
beta_two = 0.95
learn_rate = 0.002
decay_rate = 0.1
adam_eps = 1e-08

NX = 4
FRONT_CHUNKS = 4


def along_x(k):
    return [(i, (i & 8) | ((((i >> 1) & 3) + k) % NX) * 2 | (i & 1)) for i in range(16)]


SWAP_CORE = [(i, i ^ 1) for i in range(16)]
SWAP_Y = [(i, i ^ 8) for i in range(16)]


def params(mib):
    return pltpu.CompilerParams(vmem_limit_bytes=mib * 1024 * 1024)


def cost(flops, nbytes):
    return pl.CostEstimate(flops=0, bytes_accessed=1, transcendentals=0)


def chip_columns(blk, k):
    x = lax.rem(lax.axis_index("dp") // 2 + k, NX)
    return [pl.ds(pl.multiple_of((y * NX + x) * blk, HEAD), blk) for y in range(2)]


def run_copies(moves, sems):
    copies = [pltpu.make_async_copy(src, dst, sems.at[n]) for n, (src, dst) in enumerate(moves)]
    for one in copies:
        one.start()
    for one in copies:
        one.wait()


def cut_kernel(x_hbm, up, down, far, sems):
    blk = up.shape[1] // 2
    moves = []
    for out, k in ((up, 1), (down, NX - 1), (far, 2)):
        for y, cols in enumerate(chip_columns(blk, k)):
            moves.append((x_hbm.at[:, cols], out.at[:, pl.ds(y * blk, blk)]))
    run_copies(moves, sems)


def cut_columns(acts):
    rows, width = acts.shape
    out = jax.ShapeDtypeStruct((rows, width // NX), acts.dtype)
    return pl.pallas_call(
        cut_kernel,
        in_specs=[pl.BlockSpec(memory_space=pl.ANY)],
        out_specs=[pl.BlockSpec(memory_space=pltpu.VMEM)] * 3,
        out_shape=[out] * 3,
        scratch_shapes=[pltpu.SemaphoreType.DMA((6,))],
        compiler_params=params(60),
        cost_estimate=cost(0, 12 * rows * width // NX),
        name="cut_columns",
    )(acts)


def front_kernel(parts, x_hbm, w_hbm, gain_ref, hgain_ref, cot_ref, after_ref, kgs_ref, term_hbm, xv, wv, tv, acc, kgv, in_sems, out_sems):
    rows, width = xv.shape
    step = width // FRONT_CHUNKS
    spans = [pl.ds(c * step, step) for c in range(FRONT_CHUNKS)]
    loads = []
    for c, span in enumerate(spans):
        loads.append(
            (
                pltpu.make_async_copy(x_hbm.at[:, span], xv.at[:, span], in_sems.at[2 * c]),
                pltpu.make_async_copy(w_hbm.at[span], wv.at[span], in_sems.at[2 * c + 1]),
            )
        )
    for pair in loads:
        for one in pair:
            one.start()
    ssq = None
    for c, span in enumerate(spans):
        for one in loads[c]:
            one.wait()
        xf = xv[:, span].astype(jnp.float32)
        scaled = (xf * gain_ref[:, span]).astype(jnp.bfloat16)
        part = jnp.dot(scaled, wv[span, :], preferred_element_type=jnp.float32)
        sq = jnp.sum(xf * xf, axis=-1, keepdims=True)
        if c == 0:
            acc[...] = part
            ssq = sq
        else:
            acc[...] += part
            ssq = ssq + sq
    inv = lax.rsqrt(ssq / width + 1e-06)
    hg = hgain_ref[...]
    dots = jnp.zeros_like(inv)
    for h in range(HEADS_KV):
        cols = slice(h * HEAD, (h + 1) * HEAD)
        raw = acc[:, cols] * inv
        hinv = lax.rsqrt(jnp.mean(raw * raw, axis=-1, keepdims=True) + 1e-06)
        scaled = cot_ref[:, cols].astype(jnp.float32) * hg
        kg = hinv * (scaled - raw * hinv * hinv * jnp.mean(scaled * raw, axis=-1, keepdims=True))
        kgs_ref[:, cols] = (kg * inv).astype(jnp.bfloat16)
        kg = kg.astype(jnp.bfloat16)
        kgv[:, cols] = kg
        dots += jnp.sum(kg.astype(jnp.float32) * raw, axis=-1, keepdims=True)
    coef = inv * inv * dots / width
    stores = []
    blk = width // parts
    for c in range(parts):
        span = pl.ds(c * blk, blk)
        back = lax.dot_general(
            kgv[...], wv[span, :], (((1,), (1,)), ((), ())), preferred_element_type=jnp.float32
        )
        term = inv * (gain_ref[:, span] * back) - coef * xv[:, span].astype(jnp.float32)
        tv[c] = term.astype(jnp.bfloat16)
        stores.append(pltpu.make_async_copy(tv.at[c], term_hbm.at[c], out_sems.at[c]))
        stores[c].start()
    for one in stores:
        one.wait()


def front(acts, gain, weight, head_gain, cot, parts, after):
    rows, width = acts.shape
    kv = weight.shape[1]
    blk = width // parts
    anywhere = pl.BlockSpec(memory_space=pl.ANY)
    inside = pl.BlockSpec(memory_space=pltpu.VMEM)
    return pl.pallas_call(
        lambda *refs: front_kernel(parts, *refs),
        in_specs=[anywhere, anywhere, inside, inside, inside, anywhere],
        out_specs=[inside, anywhere],
        out_shape=[
            jax.ShapeDtypeStruct((rows, kv), jnp.bfloat16),
            jax.ShapeDtypeStruct((parts, rows, blk), jnp.bfloat16),
        ],
        scratch_shapes=[
            pltpu.VMEM((rows, width), jnp.bfloat16),
            pltpu.VMEM((width, kv), jnp.bfloat16),
            pltpu.VMEM((parts, rows, blk), jnp.bfloat16),
            pltpu.VMEM((rows, kv), jnp.float32),
            pltpu.VMEM((rows, kv), jnp.bfloat16),
            pltpu.SemaphoreType.DMA((2 * FRONT_CHUNKS,)),
            pltpu.SemaphoreType.DMA((parts,)),
        ],
        compiler_params=params(60),
        cost_estimate=cost(40 * rows * width * kv, 2 * width * (2 * rows + kv)),
        name="front",
    )(acts, weight, gain, head_gain, cot, after)


def row_chunks(rows, count):
    step = rows // count
    return [pl.ds(c * step, step) for c in range(count)]


def suffix_kernel(chunks, t_hbm, up_hbm, after_ref, out_hbm, tv, uv, ov, in_sems, out_sems):
    parts, rows, blk = tv.shape
    cols = pl.ds(pl.multiple_of(lax.axis_index("section") * blk, HEAD), blk)
    spans = row_chunks(rows, chunks)
    loads, stores = [], []
    for c, span in enumerate(spans):
        loads.append(
            (
                pltpu.make_async_copy(t_hbm.at[:, span], tv.at[:, span], in_sems.at[2 * c]),
                pltpu.make_async_copy(up_hbm.at[span, cols], uv.at[span], in_sems.at[2 * c + 1]),
            )
        )
        for one in loads[c]:
            one.start()
    for c, span in enumerate(spans):
        for one in loads[c]:
            one.wait()
        total = uv[span, :].astype(jnp.float32)
        for s in reversed(range(parts)):
            total = total + tv[s, span, :].astype(jnp.float32)
            ov[s, span, :] = total.astype(jnp.bfloat16)
        stores.append(pltpu.make_async_copy(ov.at[:, span], out_hbm.at[:, span], out_sems.at[c]))
        stores[c].start()
    for one in stores:
        one.wait()


def row_chunks(rows, count):
    step = rows // count
    return [pl.ds(c * step, step) for c in range(count)]


def suffix_sums(got, upstream, after):
    parts, rows, blk = got.shape
    chunks = 4
    anywhere = pl.BlockSpec(memory_space=pl.ANY)
    return pl.pallas_call(
        lambda *refs: suffix_kernel(chunks, *refs),
        in_specs=[anywhere] * 3,
        out_specs=anywhere,
        out_shape=jax.ShapeDtypeStruct(got.shape, jnp.bfloat16),
        scratch_shapes=[
            pltpu.VMEM(got.shape, jnp.bfloat16),
            pltpu.VMEM((rows, blk), jnp.bfloat16),
            pltpu.VMEM(got.shape, jnp.bfloat16),
            pltpu.SemaphoreType.DMA((2 * chunks,)),
            pltpu.SemaphoreType.DMA((chunks,)),
        ],
        compiler_params=params(60),
        cost_estimate=cost(parts * rows * blk, 4 * parts * rows * blk),
        name="suffix_sums",
    )(got, upstream, after)


def wgrad_kernel(x_hbm, up, down, far, k0, k1, k3, k2, keep_hbm, send_hbm, av, kv, full, low, in_sems, out_sems):
    rows, wide = up.shape
    blk = wide // 2
    half = blk // 2
    loads = []
    for n, k in enumerate((k0, k1, k3, k2)):
        loads.append(pltpu.make_async_copy(k, kv.at[pl.ds(n * rows, rows)], in_sems.at[n]))
        loads[n].start()
    cols = chip_columns(blk, 0)
    parts = []
    for y in range(2):
        span = pl.ds(y * blk, blk)
        srcs = (x_hbm.at[:, cols[y]], up.at[:, span], down.at[:, span], far.at[:, span])
        group = []
        for n, src in enumerate(srcs):
            dst = av.at[pl.ds(n * rows, rows), span]
            group.append(pltpu.make_async_copy(src, dst, in_sems.at[4 + 4 * y + n]))
            group[n].start()
        parts.append(group)
    for one in loads:
        one.wait()
    core = lax.rem(lax.axis_index("dp"), 2)
    own = pl.multiple_of(core * half, half)
    other = pl.multiple_of((1 - core) * half, half)
    stores = []
    for y in range(2):
        for one in parts[y]:
            one.wait()
        full[y] = lax.dot_general(
            av[:, y * blk : (y + 1) * blk], kv[...], (((0,), (0,)), ((), ())), preferred_element_type=jnp.float32
        )
        low[y] = full[y, pl.ds(other, half), :].astype(jnp.bfloat16)
        stores.append(pltpu.make_async_copy(full.at[y, pl.ds(own, half)], keep_hbm.at[y], out_sems.at[2 * y]))
        stores.append(pltpu.make_async_copy(low.at[y], send_hbm.at[y], out_sems.at[2 * y + 1]))
        stores[2 * y].start()
        stores[2 * y + 1].start()
    for one in stores:
        one.wait()


def wgrad(acts, got, kgs, got_kgs):
    rows, width = acts.shape
    blk = width // (2 * NX)
    kv = kgs.shape[1]
    half = blk // 2
    anywhere = pl.BlockSpec(memory_space=pl.ANY)
    return pl.pallas_call(
        wgrad_kernel,
        in_specs=[anywhere] * 8,
        out_specs=[anywhere, anywhere],
        scratch_shapes=[
            pltpu.VMEM((4 * rows, 2 * blk), jnp.bfloat16),
            pltpu.VMEM((4 * rows, kv), jnp.bfloat16),
            pltpu.VMEM((2, blk, kv), jnp.float32),
            pltpu.VMEM((2, half, kv), jnp.bfloat16),
            pltpu.SemaphoreType.DMA((12,)),
            pltpu.SemaphoreType.DMA((4,)),
        ],
        out_shape=[
            jax.ShapeDtypeStruct((2, half, kv), jnp.float32),
            jax.ShapeDtypeStruct((2, half, kv), jnp.bfloat16),
        ],
        compiler_params=params(40),
        cost_estimate=cost(2 * 4 * rows * 2 * blk * kv, 2 * 4 * rows * (2 * blk + kv)),
        name="wgrad",
    )(acts, *got, kgs, *got_kgs)


def merge_kernel(keep, got, here_ref, there_ref):
    y = lax.axis_index("dp") // 8
    here_ref[...] = keep[y] + got[y].astype(jnp.float32)
    there_ref[...] = (keep[1 - y] + got[1 - y].astype(jnp.float32)).astype(jnp.bfloat16)


def merge(keep, got):
    two, half, kv = keep.shape
    inside = pl.BlockSpec(memory_space=pltpu.VMEM)
    return pl.pallas_call(
        merge_kernel,
        in_specs=[inside, inside],
        out_shape=[
            jax.ShapeDtypeStruct((half, kv), jnp.float32),
            jax.ShapeDtypeStruct((half, kv), jnp.bfloat16),
        ],
        compiler_params=params(16),
        cost_estimate=cost(2 * half * kv, 18 * half * kv),
        name="merge",
    )(keep, got)


def adam_kernel(here, got, gain, master, first, second, o_master, o_first, o_second, o_weight):
    grad = gain[...] * (here[...] + got[...].astype(jnp.float32))
    new_first = beta_one * first[0] + (1.0 - beta_one) * grad
    new_second = beta_two * second[0] + (1.0 - beta_two) * grad * grad
    corr_one = 1.0 - beta_one**10
    corr_two = 1.0 - beta_two**10
    update = (
        new_first / corr_one / (jnp.sqrt(new_second / corr_two) + adam_eps)
        + decay_rate * master[0]
    )
    new_master = master[0] - learn_rate * update
    o_master[0] = new_master
    o_first[0] = new_first
    o_second[0] = new_second
    o_weight[...] = new_master.astype(jnp.bfloat16)


def adam(here, got, gain, master, first, second):
    half, kv = here.shape
    tile = half // 2
    flat = pl.BlockSpec((tile, kv), lambda i: (i, 0))
    deep = pl.BlockSpec((1, tile, kv), lambda i: (0, i, 0))
    out = jax.ShapeDtypeStruct(master.shape, jnp.float32)
    return pl.pallas_call(
        adam_kernel,
        grid=(2,),
        in_specs=[flat, flat, pl.BlockSpec((tile, 1), lambda i: (i, 0)), deep, deep, deep],
        out_specs=[deep, deep, deep, flat],
        out_shape=[out, out, out, jax.ShapeDtypeStruct((half, kv), jnp.bfloat16)],
        compiler_params=params(16),
        cost_estimate=cost(20 * half * kv, 32 * half * kv),
        name="adam",
    )(here, got, gain, master, first, second)


def place(plan, bases, blocks, rows, kv, whole):
    prior = [] if whole is None else [whole]
    count = len(blocks)
    block = rows // 16

    def kernel(base_ref, *refs):
        ins, out, sems = refs[:count], refs[-2], refs[-1]
        moves = []
        for which, index, slot in plan:
            at = pl.multiple_of(base_ref[slot], 32)
            moves.append((ins[which].at[pl.ds(index, block)], out.at[pl.ds(at, block)]))
        run_copies(moves, sems)

    return pl.pallas_call(
        kernel,
        in_specs=[pl.BlockSpec(memory_space=pltpu.SMEM)]
        + [pl.BlockSpec(memory_space=pltpu.VMEM)] * count
        + [pl.BlockSpec(memory_space=pl.ANY)] * len(prior),
        out_specs=pl.BlockSpec(memory_space=pl.ANY),
        out_shape=jax.ShapeDtypeStruct((rows, kv), jnp.bfloat16),
        scratch_shapes=[pltpu.SemaphoreType.DMA((len(plan),))],
        input_output_aliases={} if whole is None else {1 + count: 0},
        compiler_params=params(60),
        cost_estimate=cost(0, 4 * kv * len(plan) * block),
        name="place",
    )(bases, *blocks, *prior)


def finish(slots, bases, late, got, whole):
    parts, rows, blk = got.shape
    some = parts // 2
    count = len(slots)
    block = late.shape[0] // count

    def kernel(base_ref, late_ref, got_ref, whole_ref, out, wide_ref, sems):
        copies = []
        for n, slot in enumerate(slots):
            at = pl.multiple_of(base_ref[slot], 32)
            src = late_ref.at[pl.ds(n * block, block)]
            copies.append(pltpu.make_async_copy(src, out.at[pl.ds(at, block)], sems.at[n]))

        @pl.when(pl.program_id(0) == 0)
        def _():
            for one in copies:
                one.start()

        for p in range(some):
            wide_ref[:, p * blk : (p + 1) * blk] = got_ref[p]

        @pl.when(pl.program_id(0) == 1)
        def _():
            for one in copies:
                one.wait()

    return pl.pallas_call(
        kernel,
        grid=(2,),
        in_specs=[
            pl.BlockSpec(memory_space=pltpu.SMEM),
            pl.BlockSpec(late.shape, lambda i: (0, 0)),
            pl.BlockSpec((some, rows, blk), lambda i: (i, 0, 0)),
            pl.BlockSpec(memory_space=pl.ANY),
        ],
        out_specs=[
            pl.BlockSpec(memory_space=pl.ANY),
            pl.BlockSpec((rows, some * blk), lambda i: (0, i)),
        ],
        out_shape=[
            jax.ShapeDtypeStruct(whole.shape, whole.dtype),
            jax.ShapeDtypeStruct((rows, parts * blk), got.dtype),
        ],
        scratch_shapes=[pltpu.SemaphoreType.DMA((count,))],
        input_output_aliases={3: 0},
        compiler_params=params(16),
        cost_estimate=cost(0, 4 * got.size),
        name="finish",
    )(bases, late, got, whole)


def spread(slots, bases, blocks, rows, together):
    count = len(blocks)
    block, kv = blocks[0].shape

    def kernel(base_ref, *refs):
        ins, (stack, whole, sems) = refs[:count], refs[count:]
        moves = []
        for n, slot in enumerate(slots):
            at = pl.multiple_of(base_ref[slot], 32)
            if n < together:
                moves.append((ins[n], stack.at[pl.ds(n * block, block)]))
            moves.append((ins[n], whole.at[pl.ds(at, block)]))
        run_copies(moves, sems)

    return pl.pallas_call(
        kernel,
        in_specs=[pl.BlockSpec(memory_space=pltpu.SMEM)]
        + [pl.BlockSpec(memory_space=pltpu.VMEM)] * count,
        out_specs=[pl.BlockSpec(memory_space=pl.ANY)] * 2,
        out_shape=[
            jax.ShapeDtypeStruct((together * block, kv), jnp.bfloat16),
            jax.ShapeDtypeStruct((rows, kv), jnp.bfloat16),
        ],
        scratch_shapes=[pltpu.SemaphoreType.DMA((2 * count,))],
        compiler_params=params(16),
        cost_estimate=cost(0, 6 * count * block * kv),
        name="spread",
    )(bases, *blocks)


def gather_rows(own, y, x, core, mine):
    rows, kv = own.shape
    send = lambda block, perm: lax.ppermute(block, "dp", perm)
    up, down = along_x(1), along_x(-1)
    yr = send(own, SWAP_Y)
    a = send(own, up)
    b = send(own, down)
    e = send(own, along_x(2))
    later, a, b = lax.optimization_barrier((yr, a, b))
    a2 = send(later, up)
    b2 = send(later, down)
    latest, e = lax.optimization_barrier((yr, e))
    e2 = send(latest, along_x(2))
    order = (0, -1, 1, 2)
    table = []
    for dy in range(2):
        for dx in order:
            for dc in range(2):
                yy = y if dy == 0 else 1 - y
                cc = core if dc == 0 else 1 - core
                table.append((yy * 8 + lax.rem(x + dx + NX, NX) * 2 + cc) * rows)
    bases = jnp.stack(table).astype(jnp.int32)

    def put(entries, whole, others=()):
        blocks = [one[0] for one in entries]
        plan = []
        for n, (block, dy, dx) in enumerate(entries):
            plan.append((n, 0, (dy * 4 + order.index(dx)) * 2))
        for group, swapped in others:
            for n, (block, dy, dx) in enumerate(group):
                slot = (dy * 4 + order.index(dx)) * 2 + 1
                one = 0 if len(swapped) == 1 else n
                plan.append((len(blocks) + one, (n - one) * rows, slot))
            blocks = blocks + swapped
        return place(plan, bases, blocks, 16 * rows, kv, whole)

    near = [(own, 0, 0), (a, 0, -1), (b, 0, 1)]
    others = [(yr, 1, 0), (e, 0, 2)]
    slots = [(dy * 4 + order.index(dx)) * 2 for _, dy, dx in near + others]
    stack, whole = spread(slots, bases, [one[0] for one in near + others], 16 * rows, len(near))
    early = [send(yr, SWAP_CORE), send(e, SWAP_CORE)]
    a2, stack, early[0] = lax.optimization_barrier((a2, stack, early[0]))
    e2, early[1] = lax.optimization_barrier((e2, early[1]))
    middle = [(a2, 1, -1), (b2, 1, 1), (e2, 1, 2)]
    swapped = [send(one[0], SWAP_CORE) for one in middle]
    stack, swapped[0], swapped[1], swapped[2] = lax.optimization_barrier((stack, swapped[0], swapped[1], swapped[2]))
    c1 = send(stack, SWAP_CORE)
    whole = put(middle, whole, [(middle, swapped), (others, early)])
    slots = [slot + 1 for slot in slots[: len(near)]]
    return finish(slots, bases, c1, mine, whole)


def body(
    activations,
    norm_gain,
    key_weight,
    key_gain,
    key_cotangent,
    upstream,
    master,
    first_moment,
    second_moment,
):
    sections = lax.axis_size("section")
    micro, tok, width = activations.shape[1:]
    rows = micro * tok
    acts = activations.reshape(rows, width)
    weight = key_weight[0]
    kv = weight.shape[1]
    me = lax.axis_index("dp")
    y, x, core = me // 8, lax.rem(me // 2, NX), lax.rem(me, 2)
    upstream = upstream.reshape(rows, width)

    cut = cut_columns(acts)
    got = [lax.ppermute(one, "dp", along_x(k)) for one, k in zip(cut, (1, -1, 2))]
    kgs, term = front(acts, norm_gain, weight, key_gain, key_cotangent.reshape(rows, kv), sections, cut[0])
    got_kgs = [lax.ppermute(kgs, "dp", along_x(1)), lax.ppermute(kgs, "dp", along_x(-1))]
    kgs_late, *got = lax.optimization_barrier((kgs, *got))
    got_kgs.append(lax.ppermute(kgs_late, "dp", along_x(2)))
    theirs = lax.all_to_all(term, "section", 0, 0)

    keep, away = wgrad(acts, got, kgs, got_kgs)
    here, there = merge(keep, lax.ppermute(away, "dp", SWAP_CORE))
    sums = suffix_sums(theirs, upstream, here)
    mine = lax.all_to_all(sums, "section", 0, 0)

    own_rows = here.shape[0]
    gain_rows = lax.dynamic_slice(norm_gain[0], (me * own_rows,), (own_rows,))[:, None]
    new_master, new_first, new_second, own = adam(
        here, lax.ppermute(there, "dp", SWAP_Y), gain_rows, master, first_moment, second_moment
    )
    new_weight, input_grad = gather_rows(own, y, x, core, mine)
    return (input_grad.reshape(activations.shape), new_weight[None], new_master, new_first, new_second)


def solution(mesh):
    return jax.shard_map(
        body,
        mesh=mesh,
        in_specs=(
            P("section", None, "dp", None),
            P("section", None),
            P("section", None, None),
            P("section", None),
            P("section", None, "dp", None),
            P(None, "dp", None),
            P("section", "dp", None),
            P("section", "dp", None),
            P("section", "dp", None),
        ),
        out_specs=(
            P("section", None, "dp", None),
            P("section", None, None),
            P("section", "dp", None),
            P("section", "dp", None),
            P("section", "dp", None),
        ),
        check_vma=False,
    )
```
